256 devices in a mesh: plane: 128 (over x, y, z), rad: 2 (over core).
Axes of the slice: x: 4, y: 4, z: 8, core: 2. Of those that a mesh axis runs over, the one named last changes fastest.
Arguments:
- coefficients: float32 [3, 128, 768, 256], P(None, 'plane', None, 'rad'), may hold values from -18 to 18
Outputs:
- convection: float32 [3, 128, 768, 256], P(None, 'plane', None, 'rad')
- stress: bfloat16 [6, 128, 768, 256], P(None, 'plane', None, 'rad')
The draws below stay inside these ranges and needn't reach their ends.
All inputs are finite; a program needn't handle non-finite values.
Results may differ from the reference program's by a relative error of at most 0.0033.
Values sent between devices are 32-bit elements; how exact they have to be, the bound alone decides.
A program may use at most 128 MiB of HBM per device.

```python
import math
import jax
import jax.numpy as jnp
from jax import lax

NZ = 128
NT = 768
NR = 256


def draw_coefficients(key, part):
    key = jax.random.fold_in(key, 7)
    noise_key, plane_key, angle_key = jax.random.split(key, 3)
    degree_real = jnp.arange(NR, dtype=jnp.float32)
    decay = 1.0 / ((1.0 + degree_real) * (1.0 + degree_real))
    noise = jnp.clip(jax.random.normal(noise_key, (3, NZ, NT, NR), jnp.float32), -6.0, 6.0)
    plane_scale = jnp.exp(jax.random.uniform(plane_key, (NZ,), jnp.float32, 0.0, 0.5 * math.log(10.0)))
    angle_scale = jnp.exp(jax.random.uniform(angle_key, (NT,), jnp.float32, 0.0, 0.5 * math.log(10.0)))
    return 0.3 * noise * decay * plane_scale[None, :, None, None] * angle_scale[None, None, :, None]


def setup_inputs(seed: int = 0) -> dict:
    keys = jax.random.split(jax.random.key(seed), 2)
    return {
        "coefficients": draw_coefficients(jax.random.fold_in(keys[1], 71), 0),
    }


inner_radius = 1.0
outer_radius = 1.4
axial_factor = 3.0
step_time = 0.002
component_pairs = ((0, 0), (1, 1), (2, 2), (0, 1), (0, 2), (1, 2))
pair_weights = (1.0, 1.0, 1.0, 2.0, 2.0, 2.0)

def chebyshev_tables(points):
    middle = 0.5 * (inner_radius + outer_radius)
    half_gap = 0.5 * (outer_radius - inner_radius)
    degree = jnp.arange(points, dtype=jnp.int32)
    phases = jnp.mod(degree[:, None] * degree[None, :], 2 * (points - 1))
    angles = jnp.pi * phases.astype(jnp.float32) / (points - 1)
    values = jnp.cos(angles)
    node_angles = jnp.pi * degree.astype(jnp.float32) / (points - 1)
    node_sines = jnp.sin(node_angles)
    inside = (degree > 0) & (degree < points - 1)
    safe_sines = jnp.where(inside, node_sines, 1.0)
    degree_real = degree.astype(jnp.float32)[:, None]
    squares = degree_real * degree_real
    parity = jnp.where(jnp.mod(degree, 2) == 0, -1.0, 1.0)[:, None]
    edges = jnp.where(degree[None, :] == 0, squares, parity * squares)
    slopes = jnp.where(inside[None, :], degree_real * jnp.sin(angles) / safe_sines[None, :], edges) / half_gap
    radius = middle + half_gap * jnp.cos(node_angles)
    return (values, slopes, radius)

def spectral_slope(field, axis, factor):
    points = field.shape[axis]
    spectrum = jnp.fft.rfft(field, axis=axis)
    wavenumbers = jnp.arange(points // 2 + 1)
    multiplier = jnp.where(wavenumbers == points // 2, 0.0, factor * wavenumbers)
    layout = [1] * field.ndim
    layout[axis] = points // 2 + 1
    spectrum = spectrum * (1j * multiplier).reshape(layout)
    return jnp.fft.irfft(spectrum, n=points, axis=axis)

def spectral_cut(field, axis, keep):
    points = field.shape[axis]
    spectrum = jnp.fft.rfft(field, axis=axis)
    layout = [1] * field.ndim
    layout[axis] = points // 2 + 1
    keepers = (jnp.arange(points // 2 + 1) < keep).reshape(layout)
    spectrum = jnp.where(keepers, spectrum, 0.0)
    return jnp.fft.irfft(spectrum, n=points, axis=axis)

def pair_products(velocity):
    return jnp.stack([velocity[couple[0]] * velocity[couple[1]] for couple in component_pairs])

def strain_rate(velocity, radial, angular, axial, radius):
    inverse = 1.0 / radius
    strain = jnp.stack([radial[0], angular[1] * inverse + velocity[0] * inverse, axial[2], 0.5 * (radial[1] - velocity[1] * inverse + angular[0] * inverse), 0.5 * (axial[0] + radial[2]), 0.5 * (axial[1] + angular[2] * inverse)])
    weights = jnp.asarray(pair_weights, dtype=jnp.float32).reshape(6, 1, 1, 1)
    magnitude = jnp.sqrt(2.0 * lax.optimization_barrier(jnp.sum(weights * strain * strain, axis=0)))
    return (strain, magnitude)

def advection(velocity, radial, angular, axial, radius):
    inverse = 1.0 / radius
    carried = velocity[1] * inverse
    radial_part = velocity[0] * radial[0] + carried * angular[0] + velocity[2] * axial[0] - velocity[1] * carried
    swirl_part = velocity[0] * radial[1] + carried * angular[1] + velocity[2] * axial[1] + velocity[0] * carried
    axial_part = velocity[0] * radial[2] + carried * angular[2] + velocity[2] * axial[2]
    return jnp.stack([radial_part, swirl_part, axial_part])

def shell_terms(filtered):
    mean_velocity = filtered[0:3]
    mean_products = filtered[3:9]
    mean_strain = filtered[9:15]
    mean_scaled = filtered[15:21]
    weights = jnp.asarray(pair_weights, dtype=jnp.float32).reshape(6, 1, 1, 1)
    leonard = mean_products - pair_products(mean_velocity)
    mean_magnitude = jnp.sqrt(2.0 * lax.optimization_barrier(jnp.sum(weights * mean_strain * mean_strain, axis=0)))
    model = 2.0 * (mean_scaled - 4.0 * mean_magnitude[None] * mean_strain)
    cross_sum = lax.optimization_barrier(jnp.sum(weights * leonard * model, axis=(0, 1, 2)))
    model_sum = lax.optimization_barrier(jnp.sum(weights * model * model, axis=(0, 1, 2)))
    return (cross_sum, model_sum)

def reference(coefficients):
    values, slopes, radius = chebyshev_tables(NR)
    width = math.gcd(NR, 16)

    def one_block(begin):
        columns = lax.dynamic_slice_in_dim(values, begin, width, 1)
        derived = lax.dynamic_slice_in_dim(slopes, begin, width, 1)
        local_radius = lax.dynamic_slice_in_dim(radius, begin, width, 0)
        velocity = jnp.einsum('cztk,kj->cztj', coefficients, columns, precision=lax.Precision.HIGHEST)
        radial = jnp.einsum('cztk,kj->cztj', coefficients, derived, precision=lax.Precision.HIGHEST)
        angular = spectral_slope(velocity, 2, 1.0)
        axial = spectral_slope(velocity, 1, axial_factor)
        strain, magnitude = strain_rate(velocity, radial, angular, axial, local_radius)
        scaled = magnitude[None] * strain
        products = jnp.concatenate([velocity, pair_products(velocity), strain, scaled], 0)
        filtered = spectral_cut(spectral_cut(products, 2, NT // 4), 1, NZ // 4)
        cross_sum, model_sum = shell_terms(filtered)
        points = NZ * NT
        coefficient = cross_sum / points / (model_sum / points + 1e-06)
        stress = (-2.0 * coefficient * scaled).astype(jnp.bfloat16)
        convection = -step_time * advection(velocity, radial, angular, axial, local_radius)
        return (convection, stress)
    starts = jnp.arange(NR // width, dtype=jnp.int32) * width
    convection, stress = lax.map(one_block, starts)
    convection = jnp.moveaxis(convection, 0, 3).reshape(3, NZ, NT, NR)
    stress = jnp.moveaxis(stress, 0, 3).reshape(6, NZ, NT, NR)
    return (convection, stress)
```

```python
import functools

import jax
import jax.numpy as jnp
import ml_dtypes
import numpy as np
from jax import lax
from jax.experimental import pallas as pl
from jax.experimental.pallas import tpu as pltpu
from jax.sharding import PartitionSpec as P

NZ = 128
NT = 768
NR = 256
HALF = 128
FLAT = 3 * NT
KEPT = 64
FIELDS = 21

inner_radius = 1.0
outer_radius = 1.4
axial_factor = 3.0
step_time = 0.002
component_pairs = ((0, 0), (1, 1), (2, 2), (0, 1), (0, 2), (1, 2))
pair_weights = (1.0, 1.0, 1.0, 2.0, 2.0, 2.0)

MESH = pl.DeviceIdType.MESH
f32 = jnp.float32
bf16 = jnp.bfloat16


def two_parts(table):
    table = table.astype(np.float32)
    high = table.astype(ml_dtypes.bfloat16)
    low = (table - high.astype(np.float32)).astype(ml_dtypes.bfloat16)
    return (high, low)


def chebyshev_tables(points):
    degree = np.arange(points, dtype=np.int64)
    angles = np.pi * np.mod(degree[:, None] * degree[None, :], 2 * (points - 1)) / (points - 1)
    node_angles = np.pi * degree / (points - 1)
    inside = (degree > 0) & (degree < points - 1)
    sines = np.where(inside, np.sin(node_angles), 1.0)
    real = degree.astype(np.float64)[:, None]
    parity = np.where(degree % 2 == 0, -1.0, 1.0)[:, None]
    edges = np.where(degree[None, :] == 0, real * real, parity * real * real)
    half_gap = 0.5 * (outer_radius - inner_radius)
    slopes = np.where(inside[None, :], real * np.sin(angles) / sines[None, :], edges) / half_gap
    radius = 0.5 * (inner_radius + outer_radius) + half_gap * np.cos(node_angles)
    return (np.cos(angles), slopes, radius)


def slope_table(points, factor):
    offset = np.arange(points)[:, None] - np.arange(points)[None, :]
    turned = np.pi * offset / points
    diagonal = offset == 0
    sines = np.where(diagonal, 1.0, np.sin(turned))
    parity = np.where(offset % 2 == 0, 0.5, -0.5)
    return np.where(diagonal, 0.0, factor * parity * np.cos(turned) / sines)


def smooth_table(points, keep):
    offset = np.arange(points)[:, None] - np.arange(points)[None, :]
    modes = np.arange(1, keep)
    row = (1.0 + 2.0 * np.cos(2 * np.pi * np.arange(points)[:, None] * modes / points).sum(1)) / points
    return row[np.mod(offset, points)]


def kept_modes(points, keep):
    place = 2 * np.pi * np.arange(points) / points
    table = np.zeros((points, 2 * keep))
    table[:, 0] = np.sqrt(1.0 / points)
    for mode in range(1, keep):
        table[:, 2 * mode - 1] = np.sqrt(2.0 / points) * np.cos(mode * place)
        table[:, 2 * mode] = np.sqrt(2.0 / points) * np.sin(mode * place)
    return table


def all_tables():
    values, slopes, radius = chebyshev_tables(NR)
    blocks = []
    for core in range(2):
        own = slice(core * HALF, (core + 1) * HALF)
        for part in range(2):
            degrees = slice(part * HALF, (part + 1) * HALF)
            blocks += [values[degrees, own].T, slopes[degrees, own].T]
    chebyshev = np.concatenate(blocks, 0)
    modes = kept_modes(NZ, NZ // 4)
    inverse = (1.0 / radius).astype(np.float32)
    return dict(
        cheb=two_parts(chebyshev),
        angle=two_parts(slope_table(NT, 1.0)),
        smooth=two_parts(smooth_table(NT, NT // 4)),
        axis=two_parts(slope_table(NZ, axial_factor)),
        modes=two_parts(modes),
        modes_t=two_parts(np.ascontiguousarray(modes.T)),
        inverse=inverse,
    )


def split(value):
    high = value.astype(bf16)
    return (high, (value - high.astype(f32)).astype(bf16))


def dot3(a, b, by_rows=False):
    dims = (((1,), (1 if by_rows else 0,)), ((), ()))
    one = functools.partial(lax.dot_general, dimension_numbers=dims, preferred_element_type=f32)
    return one(a[0], b[0]) + (one(a[0], b[1]) + one(a[1], b[0]))


def strain_of(velocity, radial, angular, axial, inverse):
    strain = (
        radial[0],
        (angular[1] + velocity[0]) * inverse,
        axial[2],
        0.5 * (radial[1] + (angular[0] - velocity[1]) * inverse),
        0.5 * (axial[0] + radial[2]),
        0.5 * (axial[1] + angular[2] * inverse),
    )
    return (strain, magnitude_of(strain))


def magnitude_of(strain):
    straight = strain[0] * strain[0] + strain[1] * strain[1] + strain[2] * strain[2]
    mixed = strain[3] * strain[3] + strain[4] * strain[4] + strain[5] * strain[5]
    return jnp.sqrt(2.0 * (straight + 2.0 * mixed))


def peer(me, step):
    x = (me // 32 + step // 32) % 4
    y = (me // 8 % 4 + step // 8 % 4) % 4
    z = (me % 8 + step % 8) % 8
    return x * 32 + y * 8 + z


def loop(count, body):
    def step(i, carry):
        body(i)
        return carry

    lax.fori_loop(0, count, step, 0)


def kernel(
    coef, cheb_h, cheb_l, angle_h_hbm, angle_l_hbm, smooth_h_hbm, smooth_l_hbm, axis_h, axis_l, modes_h, modes_l,
    modes_t_h, modes_t_l, inverse_rows, inverse_list,
    conv_out, stress_out,
    own, other, own_h, own_l, other_h, other_l, vel_t, rad_t, vel_z, rad_z, axial_z, axial_r, vel_p, rad_p, ang_p,
    vel_h, vel_l, vz_h, vz_l, ang_z, field_h, field_l, mode_h, mode_l, filtered, scaled, conv, stress, axial_p,
    coefficient_own, coefficient_all, angle_h, angle_l, smooth_h, smooth_l,
    table_sem, in_sem, out_sem, rad_send, rad_recv, vel_send, vel_recv, slope_send, slope_recv, back_send, back_recv,
    coefficient_send, coefficient_recv,
):
    me = lax.axis_index("plane")
    core = lax.axis_index("rad")
    partner = 1 - core

    load = pltpu.make_async_copy(coef, own, in_sem)
    load.start()
    tables = [
        pltpu.make_async_copy(source, place, table_sem.at[i])
        for i, (source, place) in enumerate(
            ((angle_h_hbm, angle_h), (angle_l_hbm, angle_l), (smooth_h_hbm, smooth_h), (smooth_l_hbm, smooth_l))
        )
    ]
    for table in tables:
        table.start()
    barrier = pltpu.get_barrier_semaphore()
    pl.semaphore_signal(barrier, 1, device_id={"rad": partner}, device_id_type=MESH)

    def greet(i):
        pl.semaphore_signal(barrier, 1, device_id={"plane": peer(me, i + 1)}, device_id_type=MESH)

    loop(NZ - 1, greet)
    pl.semaphore_wait(barrier, NZ)
    exchange = pltpu.make_async_remote_copy(
        src_ref=coef, dst_ref=other, send_sem=rad_send, recv_sem=rad_recv, device_id={"rad": partner}, device_id_type=MESH
    )
    exchange.start()

    def cheb(part, first, rows):
        place = pl.ds(pl.multiple_of((core * 2 + part) * 256 + first, HALF), rows)
        return (cheb_h[place, :], cheb_l[place, :])

    def scatter(source, target, send, recv):
        local = pltpu.make_async_copy(source.at[pl.ds(me, 1)], target.at[pl.ds(me, 1)], recv)
        local.start()

        def one(i):
            d = peer(me, i + 1)
            pltpu.make_async_remote_copy(
                src_ref=source.at[pl.ds(d, 1)],
                dst_ref=target.at[pl.ds(me, 1)],
                send_sem=send,
                recv_sem=recv,
                device_id={"plane": d},
                device_id_type=MESH,
            ).start()

        loop(NZ - 1, one)

    def wait_all(target, recv):
        pltpu.make_async_copy(target, target, recv).wait()

    def wait_sent(source, send):
        most = source.at[pl.ds(0, NZ - 8)]
        pltpu.make_async_copy(most, most, send).wait()
        last = source.at[pl.ds(0, 1)]
        for _ in range(7):
            pltpu.make_async_copy(last, last, send).wait()

    load.wait()

    def own_part(i):
        rows = pl.ds(pl.multiple_of(i * 256, 256), 256)
        part = split(own[rows, :])
        own_h[rows, :], own_l[rows, :] = part
        result = dot3(cheb(core, 0, 256), part, True)
        vel_t[:, rows] = result[:HALF]
        rad_t[:, rows] = result[HALF:]

    loop(9, own_part)
    exchange.wait_recv()

    def other_velocity(i):
        rows = pl.ds(pl.multiple_of(i * 256, 256), 256)
        part = split(other[rows, :])
        other_h[rows, :], other_l[rows, :] = part
        vel_t[:, rows] += dot3(cheb(partner, 0, HALF), part, True)

    loop(9, other_velocity)
    scatter(vel_t, vel_z, vel_send, vel_recv)

    def other_slope(i):
        rows = pl.ds(pl.multiple_of(i * 256, 256), 256)
        rad_t[:, rows] += dot3(cheb(partner, HALF, HALF), (other_h[rows, :], other_l[rows, :]), True)

    loop(9, other_slope)
    scatter(rad_t, rad_z, slope_send, slope_recv)

    for c in range(3):
        lanes = slice(c * HALF, (c + 1) * HALF)

        def plane_part(i, c=c, lanes=lanes):
            rows = pl.ds(pl.multiple_of(c * NT + i * 256, 256), 256)
            place = pl.ds(pl.multiple_of(i * 256, 256), 256)
            result = dot3((own_h[rows, :], own_l[rows, :]), cheb(core, 0, 256), True)
            result += dot3((other_h[rows, :], other_l[rows, :]), cheb(partner, 0, 256), True)
            vel_p[place, lanes] = result[:, :HALF]
            rad_p[place, lanes] = result[:, HALF:]
            vel_h[place, lanes], vel_l[place, lanes] = split(result[:, :HALF])

        loop(3, plane_part)

    for table in tables:
        table.wait()

    def plane_angle(i):
        rows = pl.ds(pl.multiple_of(i * 256, 256), 256)
        ang_p[rows, :] = dot3((angle_h[rows, :], angle_l[rows, :]), (vel_h[...], vel_l[...]))

    loop(3, plane_angle)

    wait_all(vel_z, vel_recv)
    for c in range(3):

        def axial_part(i, c=c):
            lanes = pl.ds(pl.multiple_of(c * NT + i * 256, 256), 256)
            part = split(vel_z[:, lanes])
            place = pl.ds(pl.multiple_of(i * 256, 256), 256)
            vz_h[c * NZ : (c + 1) * NZ, place], vz_l[c * NZ : (c + 1) * NZ, place] = part
            axial_z[:, lanes] = dot3((axis_h[...], axis_l[...]), part)

        loop(3, axial_part)
    scatter(axial_z, axial_r, back_send, back_recv)

    def shell_angle(i):
        lanes = pl.ds(pl.multiple_of(i * 256, 256), 256)
        ang_z[:, lanes] = -dot3((vz_h[...], vz_l[...]), (angle_h[:, lanes], angle_l[:, lanes]))

    loop(3, shell_angle)
    wait_all(rad_z, slope_recv)
    inverse = inverse_list[core * HALF + me]

    def shell_products(i):
        rows = pl.ds(pl.multiple_of(i * 16, 16), 16)
        for block in range(3):
            lanes = slice(block * 256, (block + 1) * 256)
            flat = [slice(c * NT + block * 256, c * NT + (block + 1) * 256) for c in range(3)]
            velocity = [vel_z[rows, flat[c]] for c in range(3)]
            radial = [rad_z[rows, flat[c]] for c in range(3)]
            axial = [axial_z[rows, flat[c]] for c in range(3)]
            angular = [ang_z[pl.ds(pl.multiple_of(c * NZ + i * 16, 16), 16), lanes] for c in range(3)]
            strain, magnitude = strain_of(velocity, radial, angular, axial, inverse)
            fields = velocity + [velocity[a] * velocity[b] for a, b in component_pairs]
            fields += list(strain) + [magnitude * s for s in strain]
            for f, field in enumerate(fields):
                place = pl.ds(pl.multiple_of(f * NZ + i * 16, 16), 16)
                field_h[place, lanes], field_l[place, lanes] = split(field)

    loop(NZ // 16, shell_products)

    def to_modes(f):
        rows = pl.ds(pl.multiple_of(f * NZ, NZ), NZ)
        place = pl.ds(pl.multiple_of(f * KEPT, KEPT), KEPT)
        for block in range(3):
            lanes = slice(block * 256, (block + 1) * 256)
            result = dot3((modes_t_h[...], modes_t_l[...]), (field_h[rows, lanes], field_l[rows, lanes]))
            mode_h[place, lanes], mode_l[place, lanes] = split(result)

    loop(FIELDS, to_modes)

    def smooth_group(g):
        rows = pl.ds(pl.multiple_of(g * 448, 64), 448)
        for block in range(3):
            lanes = slice(block * 256, (block + 1) * 256)
            result = dot3((mode_h[rows, :], mode_l[rows, :]), (smooth_h[:, lanes], smooth_l[:, lanes]))
            field_h[rows, lanes], field_l[rows, lanes] = split(result)

    loop(3, smooth_group)

    def from_modes(f):
        rows = pl.ds(pl.multiple_of(f * NZ, NZ), NZ)
        place = pl.ds(pl.multiple_of(f * KEPT, KEPT), KEPT)
        for block in range(3):
            lanes = slice(block * 256, (block + 1) * 256)
            filtered[rows, lanes] = dot3((modes_h[...], modes_l[...]), (field_h[place, lanes], field_l[place, lanes]))

    loop(FIELDS, from_modes)

    def shell_sums(i, sums):
        cross, model_sum = sums
        for block in range(3):
            lanes = slice(block * 256, (block + 1) * 256)
            mean = [filtered[pl.ds(pl.multiple_of(f * NZ + i * 8, 8), 8), lanes] for f in range(FIELDS)]
            magnitude = magnitude_of(mean[9:15])
            for n, (a, b) in enumerate(component_pairs):
                leonard = mean[3 + n] - mean[a] * mean[b]
                model = 2.0 * (mean[15 + n] - 4.0 * (magnitude * mean[9 + n]))
                weighted = model * pair_weights[n]
                cross = cross + leonard * weighted
                model_sum = model_sum + model * weighted
        return (cross, model_sum)

    zero = jnp.zeros((8, 256), f32)
    cross, model_sum = lax.fori_loop(0, NZ // 8, shell_sums, (zero, zero))

    def total(value):
        return jnp.sum(jnp.sum(value, axis=1, keepdims=True), axis=0, keepdims=True)

    points = NZ * NT
    coefficient = (total(cross) / points) / (total(model_sum) / points + 1e-06)
    coefficient_own[...] = jnp.broadcast_to(coefficient, (8, 128))

    def share(i):
        pltpu.make_async_remote_copy(
            src_ref=coefficient_own.at[pl.ds(0, 1)],
            dst_ref=coefficient_all.at[pl.ds(me, 1)],
            send_sem=coefficient_send,
            recv_sem=coefficient_recv,
            device_id={"plane": peer(me, i + 1)},
            device_id_type=MESH,
        ).start()

    pltpu.make_async_copy(
        coefficient_own.at[pl.ds(0, 1)], coefficient_all.at[pl.ds(me, 1)], coefficient_recv
    ).start()
    loop(NZ - 1, share)

    wait_all(axial_r, back_recv)
    for c in range(3):
        for block in range(6):
            first = c * NT + block * 128
            axial_p[block * 128 : (block + 1) * 128, c * HALF : (c + 1) * HALF] = axial_r[:, first : first + 128].T
    inverse_row = inverse_rows[pl.ds(core, 1), :]

    def plane_fields(i):
        rows = pl.ds(pl.multiple_of(i * 16, 16), 16)
        velocity, radial, angular, axial = (
            [ref[rows, c * HALF : (c + 1) * HALF] for c in range(3)] for ref in (vel_p, rad_p, ang_p, axial_p)
        )
        around = jnp.broadcast_to(inverse_row, (16, HALF))
        strain, magnitude = strain_of(velocity, radial, angular, axial, around)
        carried = velocity[1] * around
        parts = [velocity[0] * radial[c] + carried * angular[c] + velocity[2] * axial[c] for c in range(3)]
        parts[0] = parts[0] - velocity[1] * carried
        parts[1] = parts[1] + velocity[0] * carried
        for c in range(3):
            conv[pl.ds(pl.multiple_of(c * NT + i * 16, 16), 16), :] = -step_time * parts[c]
        for n in range(6):
            scaled[pl.ds(pl.multiple_of(n * NT + i * 16, 16), 16), :] = magnitude * strain[n]

    loop(NT // 16, plane_fields)
    conv_copy = pltpu.make_async_copy(conv, conv_out, out_sem.at[0])
    conv_copy.start()
    wait_all(coefficient_all, coefficient_recv)
    factor = -2.0 * coefficient_all[...].T[0:1, :]

    def plane_stress(i):
        rows = pl.ds(pl.multiple_of(i * 64, 64), 64)
        stress[rows, :] = (scaled[rows, :] * jnp.broadcast_to(factor, (64, HALF))).astype(bf16)

    loop(6 * NT // 64, plane_stress)
    stress_copy = pltpu.make_async_copy(stress, stress_out, out_sem.at[1])
    stress_copy.start()

    exchange.wait_send()
    wait_sent(vel_t, vel_send)
    wait_sent(rad_t, slope_send)
    wait_sent(axial_z, back_send)
    wait_sent(coefficient_all, coefficient_send)
    conv_copy.wait()
    stress_copy.wait()


def shards(coefficients):
    tables = all_tables()
    hbm = pl.BlockSpec(memory_space=pl.ANY)
    vmem = pl.BlockSpec(memory_space=pltpu.VMEM)
    smem = pl.BlockSpec(memory_space=pltpu.SMEM)
    flat = [FLAT, HALF]
    shell = [NZ, FLAT]
    plane = [NT, 3 * HALF]
    semaphore = pltpu.SemaphoreType.DMA
    scratch = [
        (flat, f32), (flat, f32), (flat, bf16), (flat, bf16), (flat, bf16), (flat, bf16),
        (shell, f32), (shell, f32), (shell, f32), (shell, f32), (shell, f32), (shell, f32),
        (plane, f32), (plane, f32), (plane, f32), (plane, bf16), (plane, bf16),
        ([3 * NZ, NT], bf16), ([3 * NZ, NT], bf16), ([3 * NZ, NT], f32),
        ([FIELDS * NZ, NT], bf16), ([FIELDS * NZ, NT], bf16),
        ([FIELDS * KEPT, NT], bf16), ([FIELDS * KEPT, NT], bf16),
        ([FIELDS * NZ, NT], f32), ([6 * NT, HALF], f32), (flat, f32), ([6 * NT, HALF], bf16), (plane, f32),
        ([8, 128], f32), ([NZ, 128], f32),
        ([NT, NT], bf16), ([NT, NT], bf16), ([NT, NT], bf16), ([NT, NT], bf16),
    ]
    inverse = tables["inverse"]
    rows = np.zeros((8, HALF), np.float32)
    rows[:2] = inverse.reshape(2, HALF)
    operands = [coefficients.reshape(FLAT, HALF)]
    specs = [hbm]
    for name, spec in (("cheb", vmem), ("angle", hbm), ("smooth", hbm), ("axis", vmem), ("modes", vmem), ("modes_t", vmem)):
        operands += [jnp.asarray(part) for part in tables[name]]
        specs += [spec, spec]
    operands += [jnp.asarray(rows), jnp.asarray(inverse)]
    specs += [vmem, smem]
    convection, stress = pl.pallas_call(
        kernel,
        out_shape=(jax.ShapeDtypeStruct((FLAT, HALF), f32), jax.ShapeDtypeStruct((6 * NT, HALF), bf16)),
        in_specs=specs,
        out_specs=(hbm, hbm),
        scratch_shapes=[pltpu.VMEM(tuple(shape), kind) for shape, kind in scratch]
        + [semaphore((4,)), semaphore, semaphore((2,))]
        + [semaphore] * 10,
        compiler_params=pltpu.CompilerParams(collective_id=0, has_side_effects=True, vmem_limit_bytes=60 << 20),
    )(*operands)
    return (convection.reshape(3, 1, NT, HALF), stress.reshape(6, 1, NT, HALF))


def solution(mesh):
    return jax.shard_map(
        shards,
        mesh=mesh,
        in_specs=(P(None, "plane", None, "rad"),),
        out_specs=(P(None, "plane", None, "rad"), P(None, "plane", None, "rad")),
        check_vma=False,
    )
```

```python
import functools

import jax
import jax.numpy as jnp
import ml_dtypes
import numpy as np
from jax import lax
from jax.experimental import pallas as pl
from jax.experimental.pallas import tpu as pltpu
from jax.sharding import PartitionSpec as P

NZ = 128
NT = 768
NR = 256
HALF = 128
FLAT = 3 * NT
KEPT = 64
FIELDS = 21

inner_radius = 1.0
outer_radius = 1.4
axial_factor = 3.0
step_time = 0.002
component_pairs = ((0, 0), (1, 1), (2, 2), (0, 1), (0, 2), (1, 2))
pair_weights = (1.0, 1.0, 1.0, 2.0, 2.0, 2.0)

MESH = pl.DeviceIdType.MESH
f32 = jnp.float32
bf16 = jnp.bfloat16


def two_parts(table):
    table = table.astype(np.float32)
    high = table.astype(ml_dtypes.bfloat16)
    low = (table - high.astype(np.float32)).astype(ml_dtypes.bfloat16)
    return (high, low)


def chebyshev_tables(points):
    degree = np.arange(points, dtype=np.int64)
    angles = np.pi * np.mod(degree[:, None] * degree[None, :], 2 * (points - 1)) / (points - 1)
    node_angles = np.pi * degree / (points - 1)
    inside = (degree > 0) & (degree < points - 1)
    sines = np.where(inside, np.sin(node_angles), 1.0)
    real = degree.astype(np.float64)[:, None]
    parity = np.where(degree % 2 == 0, -1.0, 1.0)[:, None]
    edges = np.where(degree[None, :] == 0, real * real, parity * real * real)
    half_gap = 0.5 * (outer_radius - inner_radius)
    slopes = np.where(inside[None, :], real * np.sin(angles) / sines[None, :], edges) / half_gap
    radius = 0.5 * (inner_radius + outer_radius) + half_gap * np.cos(node_angles)
    return (np.cos(angles), slopes, radius)


def slope_table(points, factor):
    offset = np.arange(points)[:, None] - np.arange(points)[None, :]
    turned = np.pi * offset / points
    diagonal = offset == 0
    sines = np.where(diagonal, 1.0, np.sin(turned))
    parity = np.where(offset % 2 == 0, 0.5, -0.5)
    return np.where(diagonal, 0.0, factor * parity * np.cos(turned) / sines)


def smooth_table(points, keep):
    offset = np.arange(points)[:, None] - np.arange(points)[None, :]
    modes = np.arange(1, keep)
    row = (1.0 + 2.0 * np.cos(2 * np.pi * np.arange(points)[:, None] * modes / points).sum(1)) / points
    return row[np.mod(offset, points)]


def kept_modes(points, keep):
    place = 2 * np.pi * np.arange(points) / points
    table = np.zeros((points, 2 * keep))
    table[:, 0] = np.sqrt(1.0 / points)
    for mode in range(1, keep):
        table[:, 2 * mode - 1] = np.sqrt(2.0 / points) * np.cos(mode * place)
        table[:, 2 * mode] = np.sqrt(2.0 / points) * np.sin(mode * place)
    return table


def all_tables():
    values, slopes, radius = chebyshev_tables(NR)
    blocks = []
    for core in range(2):
        own = slice(core * HALF, (core + 1) * HALF)
        for part in range(2):
            degrees = slice(part * HALF, (part + 1) * HALF)
            blocks += [values[degrees, own].T, slopes[degrees, own].T]
    chebyshev = np.concatenate(blocks, 0)
    modes = kept_modes(NZ, NZ // 4)
    inverse = (1.0 / radius).astype(np.float32)
    return dict(
        cheb=two_parts(chebyshev),
        angle=two_parts(slope_table(NT, 1.0)),
        smooth=two_parts(smooth_table(NT, NT // 4)),
        axis=two_parts(slope_table(NZ, axial_factor)),
        modes=two_parts(modes),
        modes_t=two_parts(np.ascontiguousarray(modes.T)),
        inverse=inverse,
    )


def split(value):
    high = value.astype(bf16)
    return (high, (value - high.astype(f32)).astype(bf16))


def dot3(a, b, by_rows=False):
    dims = (((1,), (1 if by_rows else 0,)), ((), ()))
    one = functools.partial(lax.dot_general, dimension_numbers=dims, preferred_element_type=f32)
    return one(a[0], b[0]) + (one(a[0], b[1]) + one(a[1], b[0]))


def strain_of(velocity, radial, angular, axial, inverse):
    strain = (
        radial[0],
        (angular[1] + velocity[0]) * inverse,
        axial[2],
        0.5 * (radial[1] + (angular[0] - velocity[1]) * inverse),
        0.5 * (axial[0] + radial[2]),
        0.5 * (axial[1] + angular[2] * inverse),
    )
    return (strain, magnitude_of(strain))


def magnitude_of(strain):
    straight = strain[0] * strain[0] + strain[1] * strain[1] + strain[2] * strain[2]
    mixed = strain[3] * strain[3] + strain[4] * strain[4] + strain[5] * strain[5]
    return jnp.sqrt(2.0 * (straight + 2.0 * mixed))


def flipped(value, mask, size):
    total, bit = 0, 1
    while bit < size:
        a, b = value // bit % 2, mask // bit % 2
        total = total + (a + b - 2 * a * b) * bit
        bit *= 2
    return total


def each_peer(me, body):
    low = [flipped(me % 8, k, 8) for k in range(8)]
    own = me // 8
    for k in range(1, 8):
        body(own * 8 + low[k])

    def group(i):
        first = flipped(own, i + 1, 16) * 8
        for k in range(8):
            body(first + low[k])

    loop(NZ // 8 - 1, group)


def loop(count, body):
    def step(i, carry):
        body(i)
        return carry

    lax.fori_loop(0, count, step, 0)


def kernel(
    coef, cheb_h, cheb_l, angle_h_hbm, angle_l_hbm, smooth_h_hbm, smooth_l_hbm, axis_h, axis_l, modes_h, modes_l,
    modes_t_h, modes_t_l, inverse_rows, inverse_list,
    conv_out, scaled_out, factor_out,
    own, other, own_h, own_l, other_h, other_l, vel_t, rad_t, vel_z, rad_z, axial_z, axial_r, vel_p, rad_p, ang_p,
    vel_h, vel_l, vz_h, vz_l, ang_z, field_h, field_l, mode_h, mode_l, filtered, scaled, conv, axial_p,
    coefficient_own, coefficient_all, angle_h, angle_l, smooth_h, smooth_l,
    table_sem, in_sem, out_sem, rad_send, rad_recv, vel_send, vel_recv, slope_send, slope_recv, back_send, back_recv,
    coefficient_send, coefficient_recv, in_y, in_x,
):
    me = lax.axis_index("plane")
    core = lax.axis_index("rad")
    partner = 1 - core

    load = pltpu.make_async_copy(coef, own, in_sem)
    load.start()
    tables = [
        pltpu.make_async_copy(source, place, table_sem.at[i])
        for i, (source, place) in enumerate(
            ((angle_h_hbm, angle_h), (angle_l_hbm, angle_l), (smooth_h_hbm, smooth_h), (smooth_l_hbm, smooth_l))
        )
    ]
    for table in tables:
        table.start()
    x, y, z = me // 32, me // 8 % 4, me % 8
    along_z = [x * 32 + y * 8 + (z + k) % 8 for k in range(1, 8)]
    along_y = [x * 32 + (y + k) % 4 * 8 + z for k in range(1, 4)]
    along_x = [(x + k) % 4 * 32 + y * 8 + z for k in range(1, 4)]

    def greet(semaphore, places):
        for place in places:
            pl.semaphore_signal(semaphore, 1, device_id={"plane": place}, device_id_type=MESH)

    barrier = pltpu.get_barrier_semaphore()
    pl.semaphore_signal(barrier, 1, device_id={"rad": partner}, device_id_type=MESH)
    greet(barrier, along_z + along_y + along_x)
    pl.semaphore_wait(barrier, 14)
    exchanges = [
        pltpu.make_async_remote_copy(
            src_ref=coef.at[pl.ds(c * NT, NT)],
            dst_ref=other.at[pl.ds(c * NT, NT)],
            send_sem=rad_send.at[c],
            recv_sem=rad_recv.at[c],
            device_id={"rad": partner},
            device_id_type=MESH,
        )
        for c in range(3)
    ]
    for exchange in exchanges:
        exchange.start()
    greet(in_y, along_y)

    def cheb(part, first, rows):
        place = pl.ds(pl.multiple_of((core * 2 + part) * 256 + first, HALF), rows)
        return (cheb_h[place, :], cheb_l[place, :])

    def scatter(source, target, send, recv, lanes=slice(None)):
        local = pltpu.make_async_copy(source.at[pl.ds(me, 1), lanes], target.at[pl.ds(me, 1), lanes], recv)
        local.start()

        def one(d):
            pltpu.make_async_remote_copy(
                src_ref=source.at[pl.ds(d, 1), lanes],
                dst_ref=target.at[pl.ds(me, 1), lanes],
                send_sem=send,
                recv_sem=recv,
                device_id={"plane": d},
                device_id_type=MESH,
            ).start()

        each_peer(me, one)

    def wait_all(target, recv):
        pltpu.make_async_copy(target, target, recv).wait()

    def wait_sent(source, send):
        most = source.at[pl.ds(0, NZ - 8)]
        pltpu.make_async_copy(most, most, send).wait()
        last = source.at[pl.ds(0, 1)]
        for _ in range(7):
            pltpu.make_async_copy(last, last, send).wait()

    load.wait()

    def own_part(i):
        rows = pl.ds(pl.multiple_of(i * 256, 256), 256)
        part = split(own[rows, :])
        own_h[rows, :], own_l[rows, :] = part
        result = dot3(cheb(core, 0, 256), part, True)
        vel_t[:, rows] = result[:HALF]
        rad_t[:, rows] = result[HALF:]

    loop(3, own_part)
    pl.semaphore_wait(in_y, 3)
    greet(in_x, along_x)
    loop(6, lambda i: own_part(i + 3))

    def other_velocity(i):
        rows = pl.ds(pl.multiple_of(i * 256, 256), 256)
        part = split(other[rows, :])
        other_h[rows, :], other_l[rows, :] = part
        vel_t[:, rows] += dot3(cheb(partner, 0, HALF), part, True)

    for c in range(3):
        exchanges[c].wait_recv()
        loop(3, lambda i, c=c: other_velocity(i + 3 * c))
    pl.semaphore_wait(in_x, 3)
    scatter(vel_t, vel_z, vel_send, vel_recv)

    def other_slope(i):
        rows = pl.ds(pl.multiple_of(i * 256, 256), 256)
        rad_t[:, rows] += dot3(cheb(partner, HALF, HALF), (other_h[rows, :], other_l[rows, :]), True)

    loop(9, other_slope)
    scatter(rad_t, rad_z, slope_send, slope_recv)

    for c in range(3):
        lanes = slice(c * HALF, (c + 1) * HALF)

        def plane_part(i, c=c, lanes=lanes):
            rows = pl.ds(pl.multiple_of(c * NT + i * 256, 256), 256)
            place = pl.ds(pl.multiple_of(i * 256, 256), 256)
            result = dot3((own_h[rows, :], own_l[rows, :]), cheb(core, 0, 256), True)
            result += dot3((other_h[rows, :], other_l[rows, :]), cheb(partner, 0, 256), True)
            vel_p[place, lanes] = result[:, :HALF]
            rad_p[place, lanes] = result[:, HALF:]
            vel_h[place, lanes], vel_l[place, lanes] = split(result[:, :HALF])

        loop(3, plane_part)

    for table in tables:
        table.wait()

    def plane_angle(i):
        rows = pl.ds(pl.multiple_of(i * 256, 256), 256)
        ang_p[rows, :] = dot3((angle_h[rows, :], angle_l[rows, :]), (vel_h[...], vel_l[...]))

    loop(3, plane_angle)

    wait_all(vel_z, vel_recv)
    for block in range(3):

        def axial_part(c, block=block):
            lanes = pl.ds(pl.multiple_of(c * NT + block * 256, 256), 256)
            part = split(vel_z[:, lanes])
            rows = pl.ds(pl.multiple_of(c * NZ, NZ), NZ)
            vz_h[rows, block * 256 : (block + 1) * 256], vz_l[rows, block * 256 : (block + 1) * 256] = part
            place = pl.ds(pl.multiple_of(block * NT + c * 256, 256), 256)
            axial_z[:, place] = dot3((axis_h[...], axis_l[...]), part)

        loop(3, axial_part)
        scatter(axial_z, axial_r, back_send.at[block], back_recv.at[block], pl.ds(block * NT, NT))

    def shell_angle(i):
        lanes = pl.ds(pl.multiple_of(i * 256, 256), 256)
        ang_z[:, lanes] = -dot3((vz_h[...], vz_l[...]), (angle_h[:, lanes], angle_l[:, lanes]))

    loop(3, shell_angle)
    wait_all(rad_z, slope_recv)
    inverse = inverse_list[core * HALF + me]

    def shell_products(i):
        rows = pl.ds(pl.multiple_of(i * 16, 16), 16)
        for block in range(3):
            lanes = slice(block * 256, (block + 1) * 256)
            flat = [slice(c * NT + block * 256, c * NT + (block + 1) * 256) for c in range(3)]
            velocity = [vel_z[rows, flat[c]] for c in range(3)]
            radial = [rad_z[rows, flat[c]] for c in range(3)]
            axial = [axial_z[rows, block * NT + c * 256 : block * NT + (c + 1) * 256] for c in range(3)]
            angular = [ang_z[pl.ds(pl.multiple_of(c * NZ + i * 16, 16), 16), lanes] for c in range(3)]
            strain, magnitude = strain_of(velocity, radial, angular, axial, inverse)
            fields = velocity + [velocity[a] * velocity[b] for a, b in component_pairs]
            fields += list(strain) + [magnitude * s for s in strain]
            for f, field in enumerate(fields):
                place = pl.ds(pl.multiple_of(f * NZ + i * 16, 16), 16)
                field_h[place, lanes], field_l[place, lanes] = split(field)

    loop(NZ // 16, shell_products)

    def to_modes(f):
        rows = pl.ds(pl.multiple_of(f * NZ, NZ), NZ)
        place = pl.ds(pl.multiple_of(f * KEPT, KEPT), KEPT)
        for block in range(3):
            lanes = slice(block * 256, (block + 1) * 256)
            result = dot3((modes_t_h[...], modes_t_l[...]), (field_h[rows, lanes], field_l[rows, lanes]))
            mode_h[place, lanes], mode_l[place, lanes] = split(result)

    loop(FIELDS, to_modes)

    def smooth_group(g):
        rows = pl.ds(pl.multiple_of(g * 448, 64), 448)
        for block in range(3):
            lanes = slice(block * 256, (block + 1) * 256)
            result = dot3((mode_h[rows, :], mode_l[rows, :]), (smooth_h[:, lanes], smooth_l[:, lanes]))
            field_h[rows, lanes], field_l[rows, lanes] = split(result)

    loop(3, smooth_group)

    def from_modes(f):
        rows = pl.ds(pl.multiple_of(f * NZ, NZ), NZ)
        place = pl.ds(pl.multiple_of(f * KEPT, KEPT), KEPT)
        for block in range(3):
            lanes = slice(block * 256, (block + 1) * 256)
            filtered[rows, lanes] = dot3((modes_h[...], modes_l[...]), (field_h[place, lanes], field_l[place, lanes]))

    loop(FIELDS, from_modes)

    def shell_sums(i, sums):
        cross, model_sum = sums
        for block in range(3):
            lanes = slice(block * 256, (block + 1) * 256)
            mean = [filtered[pl.ds(pl.multiple_of(f * NZ + i * 8, 8), 8), lanes] for f in range(FIELDS)]
            magnitude = magnitude_of(mean[9:15])
            for n, (a, b) in enumerate(component_pairs):
                leonard = mean[3 + n] - mean[a] * mean[b]
                model = 2.0 * (mean[15 + n] - 4.0 * (magnitude * mean[9 + n]))
                weighted = model * pair_weights[n]
                cross = cross + leonard * weighted
                model_sum = model_sum + model * weighted
        return (cross, model_sum)

    zero = jnp.zeros((8, 256), f32)
    cross, model_sum = lax.fori_loop(0, NZ // 8, shell_sums, (zero, zero))

    def total(value):
        return jnp.sum(jnp.sum(value, axis=1, keepdims=True), axis=0, keepdims=True)

    points = NZ * NT
    coefficient = (total(cross) / points) / (total(model_sum) / points + 1e-06)
    coefficient_own[...] = jnp.broadcast_to(coefficient, (8, 128))

    def share(d):
        pltpu.make_async_remote_copy(
            src_ref=coefficient_own.at[pl.ds(0, 1)],
            dst_ref=coefficient_all.at[pl.ds(me, 1)],
            send_sem=coefficient_send,
            recv_sem=coefficient_recv,
            device_id={"plane": d},
            device_id_type=MESH,
        ).start()

    pltpu.make_async_copy(
        coefficient_own.at[pl.ds(0, 1)], coefficient_all.at[pl.ds(me, 1)], coefficient_recv
    ).start()
    each_peer(me, share)

    inverse_row = inverse_rows[pl.ds(core, 1), :]

    def plane_fields(i):
        rows = pl.ds(pl.multiple_of(i * 32, 32), 32)
        velocity, radial, angular, axial = (
            [ref[rows, c * HALF : (c + 1) * HALF] for c in range(3)] for ref in (vel_p, rad_p, ang_p, axial_p)
        )
        around = jnp.broadcast_to(inverse_row, (32, HALF))
        strain, magnitude = strain_of(velocity, radial, angular, axial, around)
        carried = velocity[1] * around
        parts = [velocity[0] * radial[c] + carried * angular[c] + velocity[2] * axial[c] for c in range(3)]
        parts[0] = parts[0] - velocity[1] * carried
        parts[1] = parts[1] + velocity[0] * carried
        for c in range(3):
            conv[pl.ds(pl.multiple_of(c * NT + i * 32, 32), 32), :] = -step_time * parts[c]
        for n in range(6):
            scaled[pl.ds(pl.multiple_of(n * NT + i * 32, 32), 32), :] = magnitude * strain[n]

    for block in range(3):
        arrived = axial_r.at[:, pl.ds(block * NT, NT)]
        wait_all(arrived, back_recv.at[block])
        for c in range(3):
            for half in range(2):
                first = block * NT + c * 256 + half * 128
                rows = slice(block * 256 + half * 128, block * 256 + (half + 1) * 128)
                axial_p[rows, c * HALF : (c + 1) * HALF] = axial_r[:, first : first + 128].T
        loop(8, lambda i, block=block: plane_fields(i + 8 * block))
        for n in range(3):
            rows = pl.ds(n * NT + block * 256, 256)
            pltpu.make_async_copy(conv.at[rows], conv_out.at[rows], out_sem.at[0]).start()
        for n in range(6):
            rows = pl.ds(n * NT + block * 256, 256)
            pltpu.make_async_copy(scaled.at[rows], scaled_out.at[rows], out_sem.at[1]).start()
    wait_all(coefficient_all, coefficient_recv)
    factor_out[...] = jnp.broadcast_to(-2.0 * coefficient_all[...].T[0:1, :], (8, HALF))

    for exchange in exchanges:
        exchange.wait_send()
    wait_sent(vel_t, vel_send)
    wait_sent(rad_t, slope_send)
    for block in range(3):
        wait_sent(axial_z.at[:, pl.ds(block * NT, NT)], back_send.at[block])
    wait_sent(coefficient_all, coefficient_send)
    pltpu.make_async_copy(conv, conv_out, out_sem.at[0]).wait()
    pltpu.make_async_copy(scaled, scaled_out, out_sem.at[1]).wait()


def finish(conv_ref, scaled_ref, factor_ref, conv_out, stress_out):
    conv_out[...] = conv_ref[...]
    stress_out[...] = (scaled_ref[...] * factor_ref[0:1, :]).astype(bf16)


def shards(coefficients):
    tables = all_tables()
    hbm = pl.BlockSpec(memory_space=pl.ANY)
    vmem = pl.BlockSpec(memory_space=pltpu.VMEM)
    smem = pl.BlockSpec(memory_space=pltpu.SMEM)
    flat = [FLAT, HALF]
    shell = [NZ, FLAT]
    plane = [NT, 3 * HALF]
    semaphore = pltpu.SemaphoreType.DMA
    scratch = [
        (flat, f32), (flat, f32), (flat, bf16), (flat, bf16), (flat, bf16), (flat, bf16),
        (shell, f32), (shell, f32), (shell, f32), (shell, f32), (shell, f32), (shell, f32),
        (plane, f32), (plane, f32), (plane, f32), (plane, bf16), (plane, bf16),
        ([3 * NZ, NT], bf16), ([3 * NZ, NT], bf16), ([3 * NZ, NT], f32),
        ([FIELDS * NZ, NT], bf16), ([FIELDS * NZ, NT], bf16),
        ([FIELDS * KEPT, NT], bf16), ([FIELDS * KEPT, NT], bf16),
        ([FIELDS * NZ, NT], f32), ([6 * NT, HALF], f32), (flat, f32), (plane, f32),
        ([8, 128], f32), ([NZ, 128], f32),
        ([NT, NT], bf16), ([NT, NT], bf16), ([NT, NT], bf16), ([NT, NT], bf16),
    ]
    inverse = tables["inverse"]
    rows = np.zeros((8, HALF), np.float32)
    rows[:2] = inverse.reshape(2, HALF)
    operands = [coefficients.reshape(FLAT, HALF)]
    specs = [hbm]
    for name, spec in (("cheb", vmem), ("angle", hbm), ("smooth", hbm), ("axis", vmem), ("modes", vmem), ("modes_t", vmem)):
        operands += [jnp.asarray(part) for part in tables[name]]
        specs += [spec, spec]
    operands += [jnp.asarray(rows), jnp.asarray(inverse)]
    specs += [vmem, smem]
    conv, scaled, factor = pl.pallas_call(
        kernel,
        out_shape=(jax.ShapeDtypeStruct((FLAT, HALF), f32), jax.ShapeDtypeStruct((6 * NT, HALF), f32),
                   jax.ShapeDtypeStruct((8, HALF), f32)),
        in_specs=specs,
        out_specs=(hbm, hbm, vmem),
        scratch_shapes=[pltpu.VMEM(tuple(shape), kind) for shape, kind in scratch]
        + [semaphore((4,)), semaphore, semaphore((2,)), semaphore((3,)), semaphore((3,))]
        + [semaphore] * 4
        + [semaphore((3,)), semaphore((3,)), semaphore, semaphore]
        + [pltpu.SemaphoreType.REGULAR] * 2,
        compiler_params=pltpu.CompilerParams(collective_id=0, has_side_effects=True, vmem_limit_bytes=60 << 20),
    )(*operands)
    steps = 4
    convection, stress = pl.pallas_call(
        finish,
        grid=(steps,),
        out_shape=(jax.ShapeDtypeStruct((FLAT, HALF), f32), jax.ShapeDtypeStruct((6 * NT, HALF), bf16)),
        in_specs=[
            pl.BlockSpec((FLAT // steps, HALF), lambda i: (i, 0)),
            pl.BlockSpec((6 * NT // steps, HALF), lambda i: (i, 0)),
            pl.BlockSpec((8, HALF), lambda i: (0, 0)),
        ],
        out_specs=(
            pl.BlockSpec((FLAT // steps, HALF), lambda i: (i, 0)),
            pl.BlockSpec((6 * NT // steps, HALF), lambda i: (i, 0)),
        ),
    )(conv, scaled, factor)
    return (convection.reshape(3, 1, NT, HALF), stress.reshape(6, 1, NT, HALF))


def solution(mesh):
    return jax.shard_map(
        shards,
        mesh=mesh,
        in_specs=(P(None, "plane", None, "rad"),),
        out_specs=(P(None, "plane", None, "rad"), P(None, "plane", None, "rad")),
        check_vma=False,
    )
```

```python
import functools

import jax
import jax.numpy as jnp
import ml_dtypes
import numpy as np
from jax import lax
from jax.experimental import pallas as pl
from jax.experimental.pallas import tpu as pltpu
from jax.sharding import PartitionSpec as P

NZ = 128
NT = 768
NR = 256
HALF = 128
FLAT = 3 * NT
KEPT = 64
PIECES = 6
FIELDS = 21
EARLY = 12
early_strain = (1, 2, 5)
late_strain = (0, 3, 4)
strain_places = (12, 9, 10, 13, 14, 11)

inner_radius = 1.0
outer_radius = 1.4
axial_factor = 3.0
step_time = 0.002
component_pairs = ((0, 0), (1, 1), (2, 2), (0, 1), (0, 2), (1, 2))
pair_weights = (1.0, 1.0, 1.0, 2.0, 2.0, 2.0)

MESH = pl.DeviceIdType.MESH
f32 = jnp.float32
bf16 = jnp.bfloat16


def two_parts(table):
    table = table.astype(np.float32)
    high = table.astype(ml_dtypes.bfloat16)
    low = (table - high.astype(np.float32)).astype(ml_dtypes.bfloat16)
    return (high, low)


def chebyshev_tables(points):
    degree = np.arange(points, dtype=np.int64)
    angles = np.pi * np.mod(degree[:, None] * degree[None, :], 2 * (points - 1)) / (points - 1)
    node_angles = np.pi * degree / (points - 1)
    inside = (degree > 0) & (degree < points - 1)
    sines = np.where(inside, np.sin(node_angles), 1.0)
    real = degree.astype(np.float64)[:, None]
    parity = np.where(degree % 2 == 0, -1.0, 1.0)[:, None]
    edges = np.where(degree[None, :] == 0, real * real, parity * real * real)
    half_gap = 0.5 * (outer_radius - inner_radius)
    slopes = np.where(inside[None, :], real * np.sin(angles) / sines[None, :], edges) / half_gap
    radius = 0.5 * (inner_radius + outer_radius) + half_gap * np.cos(node_angles)
    return (np.cos(angles), slopes, radius)


def slope_table(points, factor):
    offset = np.arange(points)[:, None] - np.arange(points)[None, :]
    turned = np.pi * offset / points
    diagonal = offset == 0
    sines = np.where(diagonal, 1.0, np.sin(turned))
    parity = np.where(offset % 2 == 0, 0.5, -0.5)
    return np.where(diagonal, 0.0, factor * parity * np.cos(turned) / sines)


def smooth_table(points, keep):
    offset = np.arange(points)[:, None] - np.arange(points)[None, :]
    modes = np.arange(1, keep)
    row = (1.0 + 2.0 * np.cos(2 * np.pi * np.arange(points)[:, None] * modes / points).sum(1)) / points
    return row[np.mod(offset, points)]


def kept_modes(points, keep):
    place = 2 * np.pi * np.arange(points) / points
    table = np.zeros((points, 2 * keep))
    table[:, 0] = np.sqrt(1.0 / points)
    for mode in range(1, keep):
        table[:, 2 * mode - 1] = np.sqrt(2.0 / points) * np.cos(mode * place)
        table[:, 2 * mode] = np.sqrt(2.0 / points) * np.sin(mode * place)
    return table


def all_tables():
    values, slopes, radius = chebyshev_tables(NR)
    blocks = []
    for core in range(2):
        own = slice(core * HALF, (core + 1) * HALF)
        for part in range(2):
            degrees = slice(part * HALF, (part + 1) * HALF)
            blocks += [values[degrees, own].T, slopes[degrees, own].T]
    chebyshev = np.concatenate(blocks, 0)
    modes = kept_modes(NZ, NZ // 4)
    inverse = (1.0 / radius).astype(np.float32)
    return dict(
        cheb=two_parts(chebyshev),
        angle=two_parts(slope_table(NT, 1.0)),
        smooth=two_parts(smooth_table(NT, NT // 4)),
        axis=two_parts(slope_table(NZ, axial_factor)),
        modes=two_parts(modes),
        modes_t=two_parts(np.ascontiguousarray(modes.T)),
        inverse=inverse,
    )


def split(value):
    high = value.astype(bf16)
    return (high, (value - high.astype(f32)).astype(bf16))


def dot3(a, b, by_rows=False):
    dims = (((1,), (1 if by_rows else 0,)), ((), ()))
    one = functools.partial(lax.dot_general, dimension_numbers=dims, preferred_element_type=f32)
    return one(a[0], b[0]) + (one(a[0], b[1]) + one(a[1], b[0]))


def strain_of(velocity, radial, angular, axial, inverse):
    late = (None, None, None)
    if radial is not None:
        late = (
            radial[0],
            0.5 * (radial[1] + (angular[0] - velocity[1]) * inverse),
            0.5 * (axial[0] + radial[2]),
        )
    return (
        late[0],
        (angular[1] + velocity[0]) * inverse,
        axial[2],
        late[1],
        late[2],
        0.5 * (axial[1] + angular[2] * inverse),
    )


def magnitude_of(strain):
    straight = strain[0] * strain[0] + strain[1] * strain[1] + strain[2] * strain[2]
    mixed = strain[3] * strain[3] + strain[4] * strain[4] + strain[5] * strain[5]
    return jnp.sqrt(2.0 * (straight + 2.0 * mixed))


def flipped(value, mask, size):
    total, bit = 0, 1
    while bit < size:
        a, b = value // bit % 2, mask // bit % 2
        total = total + (a + b - 2 * a * b) * bit
        bit *= 2
    return total


def each_peer(me, core, body):
    own = me // 8
    for k in range(1, 8):
        body(own * 8 + flipped(me % 8, k + core * (8 - 2 * k), 8))
    low = [flipped(me % 8, k + core * (7 - 2 * k), 8) for k in range(8)]

    def group(i):
        first = flipped(own, i + 1 + core * (14 - 2 * i), 16) * 8
        for k in range(8):
            body(first + low[k])

    loop(NZ // 8 - 1, group)


def loop(count, body):
    def step(i, carry):
        body(i)
        return carry

    lax.fori_loop(0, count, step, 0)


def kernel(
    coef, cheb_h, cheb_l, angle_h_hbm, angle_l_hbm, smooth_h_hbm, smooth_l_hbm, axis_h, axis_l, modes_h, modes_l,
    modes_t_h, modes_t_l, inverse_rows, inverse_list,
    conv_out, scaled_out, factor_out,
    own, other, own_h, own_l, other_h, other_l, vel_t, rad_t, vel_z, rad_z, axial_z, axial_r, vel_p, rad_p, ang_p,
    vel_h, vel_l, vz_h, vz_l, ang_z, field_h, field_l, mode_h, mode_l, smoothed_h, smoothed_l, filtered, scaled, conv, axial_p,
    coefficient_own, coefficient_all, angle_h, angle_l, smooth_h, smooth_l,
    table_sem, in_sem, out_sem, rad_send, rad_recv, vel_send, vel_recv, slope_send, slope_recv, back_send, back_recv,
    coefficient_send, coefficient_recv, in_y, in_x,
):
    me = lax.axis_index("plane")
    core = lax.axis_index("rad")
    partner = 1 - core

    load = pltpu.make_async_copy(coef, own, in_sem)
    load.start()
    tables = [
        pltpu.make_async_copy(source, place, table_sem.at[i])
        for i, (source, place) in enumerate(
            ((angle_h_hbm, angle_h), (angle_l_hbm, angle_l), (smooth_h_hbm, smooth_h), (smooth_l_hbm, smooth_l))
        )
    ]
    for table in tables:
        table.start()
    x, y, z = me // 32, me // 8 % 4, me % 8
    along_z = [x * 32 + y * 8 + (z + k) % 8 for k in range(1, 8)]
    along_y = [x * 32 + (y + k) % 4 * 8 + z for k in range(1, 4)]
    along_x = [(x + k) % 4 * 32 + y * 8 + z for k in range(1, 4)]

    def greet(semaphore, places):
        for place in places:
            pl.semaphore_signal(semaphore, 1, device_id={"plane": place}, device_id_type=MESH)

    barrier = pltpu.get_barrier_semaphore()
    pl.semaphore_signal(barrier, 1, device_id={"rad": partner}, device_id_type=MESH)
    greet(barrier, along_z + along_y + along_x)
    pl.semaphore_wait(barrier, 14)
    exchanges = [
        pltpu.make_async_remote_copy(
            src_ref=coef.at[pl.ds(c * NT, NT)],
            dst_ref=other.at[pl.ds(c * NT, NT)],
            send_sem=rad_send.at[c],
            recv_sem=rad_recv.at[c],
            device_id={"rad": partner},
            device_id_type=MESH,
        )
        for c in range(3)
    ]
    for exchange in exchanges:
        exchange.start()
    greet(in_y, along_y)

    def cheb(part, first, rows):
        place = pl.ds(pl.multiple_of((core * 2 + part) * 256 + first, HALF), rows)
        return (cheb_h[place, :], cheb_l[place, :])

    def scatter(source, target, send, recv, lanes=slice(None)):
        local = pltpu.make_async_copy(source.at[pl.ds(me, 1), lanes], target.at[pl.ds(me, 1), lanes], recv)
        local.start()

        def one(d):
            pltpu.make_async_remote_copy(
                src_ref=source.at[pl.ds(d, 1), lanes],
                dst_ref=target.at[pl.ds(me, 1), lanes],
                send_sem=send,
                recv_sem=recv,
                device_id={"plane": d},
                device_id_type=MESH,
            ).start()

        each_peer(me, core, one)

    def wait_all(target, recv):
        pltpu.make_async_copy(target, target, recv).wait()

    def wait_sent(source, send):
        most = source.at[pl.ds(0, NZ - 8)]
        pltpu.make_async_copy(most, most, send).wait()
        last = source.at[pl.ds(0, 1)]
        for _ in range(7):
            pltpu.make_async_copy(last, last, send).wait()

    load.wait()

    def own_part(i):
        rows = pl.ds(pl.multiple_of(i * 256, 256), 256)
        part = split(own[rows, :])
        own_h[rows, :], own_l[rows, :] = part
        result = dot3(cheb(core, 0, 256), part, True)
        vel_t[:, rows] = result[:HALF]
        rad_t[:, rows] = result[HALF:]

    loop(3, own_part)
    pl.semaphore_wait(in_y, 3)
    greet(in_x, along_x)
    loop(6, lambda i: own_part(i + 3))

    def other_velocity(i):
        rows = pl.ds(pl.multiple_of(i * 256, 256), 256)
        part = split(other[rows, :])
        other_h[rows, :], other_l[rows, :] = part
        vel_t[:, rows] += dot3(cheb(partner, 0, HALF), part, True)

    for c in range(3):
        exchanges[c].wait_recv()
        loop(3, lambda i, c=c: other_velocity(i + 3 * c))
        if c == 0:
            pl.semaphore_wait(in_x, 3)
        scatter(vel_t, vel_z, vel_send.at[c], vel_recv.at[c], pl.ds(c * NT, NT))

    def other_slope(i):
        rows = pl.ds(pl.multiple_of(i * 256, 256), 256)
        rad_t[:, rows] += dot3(cheb(partner, HALF, HALF), (other_h[rows, :], other_l[rows, :]), True)

    loop(9, other_slope)
    scatter(rad_t, rad_z, slope_send, slope_recv)

    for c in range(3):
        lanes = slice(c * HALF, (c + 1) * HALF)

        def plane_part(i, c=c, lanes=lanes):
            rows = pl.ds(pl.multiple_of(c * NT + i * 256, 256), 256)
            place = pl.ds(pl.multiple_of(i * 256, 256), 256)
            result = dot3((own_h[rows, :], own_l[rows, :]), cheb(core, 0, 256), True)
            result += dot3((other_h[rows, :], other_l[rows, :]), cheb(partner, 0, 256), True)
            vel_p[place, lanes] = result[:, :HALF]
            rad_p[place, lanes] = result[:, HALF:]
            vel_h[place, lanes], vel_l[place, lanes] = split(result[:, :HALF])

        loop(3, plane_part)

    for table in tables:
        table.wait()

    def plane_angle(i):
        rows = pl.ds(pl.multiple_of(i * 256, 256), 256)
        ang_p[rows, :] = dot3((angle_h[rows, :], angle_l[rows, :]), (vel_h[...], vel_l[...]))

    loop(3, plane_angle)

    for c in range(3):
        wait_all(vel_z.at[:, pl.ds(c * NT, NT)], vel_recv.at[c])

        def axial_part(block, c=c):
            lanes = pl.ds(pl.multiple_of(c * NT + block * 256, 256), 256)
            part = split(vel_z[:, lanes])
            place = pl.ds(pl.multiple_of(block * 256, 256), 256)
            vz_h[c * NZ : (c + 1) * NZ, place], vz_l[c * NZ : (c + 1) * NZ, place] = part
            place = pl.ds(pl.multiple_of(block * NT + c * 256, 256), 256)
            axial_z[:, place] = dot3((axis_h[...], axis_l[...]), part)

        loop(3, axial_part)
    for block in range(3):
        scatter(axial_z, axial_r, back_send.at[block], back_recv.at[block], pl.ds(block * NT, NT))

    def shell_angle(i):
        lanes = pl.ds(pl.multiple_of(i * 256, 256), 256)
        ang_z[:, lanes] = -dot3((vz_h[...], vz_l[...]), (angle_h[:, lanes], angle_l[:, lanes]))

    loop(3, shell_angle)
    inverse = inverse_list[core * HALF + me]

    def shell_block(i, block):
        rows = pl.ds(pl.multiple_of(i * 16, 16), 16)
        lanes = slice(block * 256, (block + 1) * 256)
        flat = [slice(c * NT + block * 256, c * NT + (block + 1) * 256) for c in range(3)]
        velocity = [vel_z[rows, flat[c]] for c in range(3)]
        axial = [axial_z[rows, block * NT + c * 256 : block * NT + (c + 1) * 256] for c in range(3)]
        angular = [ang_z[pl.ds(pl.multiple_of(c * NZ + i * 16, 16), 16), lanes] for c in range(3)]
        return rows, lanes, flat, velocity, axial, angular

    def keep(i, lanes, first, fields):
        for f, field in enumerate(fields):
            place = pl.ds(pl.multiple_of((first + f) * NZ + i * 16, 16), 16)
            field_h[place, lanes], field_l[place, lanes] = split(field)

    def early_products(i):
        for block in range(3):
            rows, lanes, flat, velocity, axial, angular = shell_block(i, block)
            strain = strain_of(velocity, None, angular, axial, inverse)
            pairs = [velocity[a] * velocity[b] for a, b in component_pairs]
            keep(i, lanes, 0, velocity + pairs + [strain[n] for n in early_strain])

    def late_products(i):
        for block in range(3):
            rows, lanes, flat, velocity, axial, angular = shell_block(i, block)
            radial = [rad_z[rows, flat[c]] for c in range(3)]
            strain = strain_of(velocity, radial, angular, axial, inverse)
            magnitude = magnitude_of(strain)
            keep(i, lanes, EARLY, [strain[n] for n in late_strain] + [magnitude * s for s in strain])

    def to_modes(f):
        rows = pl.ds(pl.multiple_of(f * NZ, NZ), NZ)
        place = pl.ds(pl.multiple_of(f * KEPT, KEPT), KEPT)
        for block in range(3):
            lanes = slice(block * 256, (block + 1) * 256)
            result = dot3((modes_t_h[...], modes_t_l[...]), (field_h[rows, lanes], field_l[rows, lanes]))
            mode_h[place, lanes], mode_l[place, lanes] = split(result)

    def smooth_rows(first, size):
        rows = pl.ds(pl.multiple_of(first, 64), size)
        for block in range(3):
            lanes = slice(block * 256, (block + 1) * 256)
            result = dot3((mode_h[rows, :], mode_l[rows, :]), (smooth_h[:, lanes], smooth_l[:, lanes]))
            smoothed_h[rows, lanes], smoothed_l[rows, lanes] = split(result)

    def from_modes(f):
        rows = pl.ds(pl.multiple_of(f * NZ, NZ), NZ)
        place = pl.ds(pl.multiple_of(f * KEPT, KEPT), KEPT)
        for block in range(3):
            lanes = slice(block * 256, (block + 1) * 256)
            filtered[rows, lanes] = dot3((modes_h[...], modes_l[...]), (smoothed_h[place, lanes], smoothed_l[place, lanes]))

    loop(NZ // 16, early_products)
    loop(EARLY, to_modes)
    loop(2, lambda g: smooth_rows(g * 384, 384))
    loop(EARLY, from_modes)
    wait_all(rad_z, slope_recv)
    loop(NZ // 16, late_products)
    loop(FIELDS - EARLY, lambda f: to_modes(EARLY + f))
    loop(3, lambda g: smooth_rows(EARLY * KEPT + g * 192, 192))
    loop(FIELDS - EARLY, lambda f: from_modes(EARLY + f))

    def shell_sums(i, sums):
        cross, model_sum = sums
        for block in range(3):
            lanes = slice(block * 256, (block + 1) * 256)
            mean = [filtered[pl.ds(pl.multiple_of(f * NZ + i * 8, 8), 8), lanes] for f in range(FIELDS)]
            strain = [mean[place] for place in strain_places]
            magnitude = magnitude_of(strain)
            for n, (a, b) in enumerate(component_pairs):
                leonard = mean[3 + n] - mean[a] * mean[b]
                model = 2.0 * (mean[15 + n] - 4.0 * (magnitude * strain[n]))
                weighted = model * pair_weights[n]
                cross = cross + leonard * weighted
                model_sum = model_sum + model * weighted
        return (cross, model_sum)

    zero = jnp.zeros((8, 256), f32)
    cross, model_sum = lax.fori_loop(0, NZ // 8, shell_sums, (zero, zero))

    def total(value):
        return jnp.sum(jnp.sum(value, axis=1, keepdims=True), axis=0, keepdims=True)

    points = NZ * NT
    coefficient = (total(cross) / points) / (total(model_sum) / points + 1e-06)
    coefficient_own[...] = jnp.broadcast_to(coefficient, (8, 128))

    def share(d):
        pltpu.make_async_remote_copy(
            src_ref=coefficient_own.at[pl.ds(0, 1)],
            dst_ref=coefficient_all.at[pl.ds(me, 1)],
            send_sem=coefficient_send,
            recv_sem=coefficient_recv,
            device_id={"plane": d},
            device_id_type=MESH,
        ).start()

    pltpu.make_async_copy(
        coefficient_own.at[pl.ds(0, 1)], coefficient_all.at[pl.ds(me, 1)], coefficient_recv
    ).start()
    each_peer(me, core, share)

    inverse_row = inverse_rows[pl.ds(core, 1), :]

    def plane_fields(i):
        rows = pl.ds(pl.multiple_of(i * 32, 32), 32)
        velocity, radial, angular, axial = (
            [ref[rows, c * HALF : (c + 1) * HALF] for c in range(3)] for ref in (vel_p, rad_p, ang_p, axial_p)
        )
        around = jnp.broadcast_to(inverse_row, (32, HALF))
        strain = strain_of(velocity, radial, angular, axial, around)
        magnitude = magnitude_of(strain)
        carried = velocity[1] * around
        parts = [velocity[0] * radial[c] + carried * angular[c] + velocity[2] * axial[c] for c in range(3)]
        parts[0] = parts[0] - velocity[1] * carried
        parts[1] = parts[1] + velocity[0] * carried
        for c in range(3):
            conv[pl.ds(pl.multiple_of(c * NT + i * 32, 32), 32), :] = -step_time * parts[c]
        for n in range(6):
            scaled[pl.ds(pl.multiple_of(n * NT + i * 32, 32), 32), :] = magnitude * strain[n]

    for block in range(3):
        arrived = axial_r.at[:, pl.ds(block * NT, NT)]
        wait_all(arrived, back_recv.at[block])
        for c in range(3):
            for half in range(2):
                first = block * NT + c * 256 + half * 128
                rows = slice(block * 256 + half * 128, block * 256 + (half + 1) * 128)
                axial_p[rows, c * HALF : (c + 1) * HALF] = axial_r[:, first : first + 128].T
        loop(8, lambda i, block=block: plane_fields(i + 8 * block))
        for n in range(3):
            rows = pl.ds(n * NT + block * 256, 256)
            pltpu.make_async_copy(conv.at[rows], conv_out.at[rows], out_sem.at[0]).start()
        for n in range(6):
            rows = pl.ds(n * NT + block * 256, 256)
            pltpu.make_async_copy(scaled.at[rows], scaled_out.at[rows], out_sem.at[1]).start()
    wait_all(coefficient_all, coefficient_recv)
    factor_out[...] = jnp.broadcast_to(-2.0 * coefficient_all[...].T[0:1, :], (8, HALF))

    for exchange in exchanges:
        exchange.wait_send()
    for c in range(3):
        wait_sent(vel_t.at[:, pl.ds(c * NT, NT)], vel_send.at[c])
    wait_sent(rad_t, slope_send)
    for block in range(3):
        wait_sent(axial_z.at[:, pl.ds(block * NT, NT)], back_send.at[block])
    wait_sent(coefficient_all, coefficient_send)
    pltpu.make_async_copy(conv, conv_out, out_sem.at[0]).wait()
    pltpu.make_async_copy(scaled, scaled_out, out_sem.at[1]).wait()


def finish(
    conv_ref, scaled_ref, factor_ref, conv_out, stress_out, conv, scaled, stress, conv_in_sem, conv_sem, in_sem, out_sem
):
    piece = 6 * NT // PIECES

    def part(i):
        return pl.ds(i * piece, piece)

    thirds = [pl.ds(c * NT, NT) for c in range(3)]
    loads = [pltpu.make_async_copy(scaled_ref.at[part(i)], scaled.at[part(i)], in_sem.at[i]) for i in range(PIECES)]
    moves = [pltpu.make_async_copy(conv_ref.at[c], conv.at[c], conv_in_sem.at[i]) for i, c in enumerate(thirds)]
    for copy in moves + loads:
        copy.start()
    copies = []
    for i, c in enumerate(thirds):
        moves[i].wait()
        copies.append(pltpu.make_async_copy(conv.at[c], conv_out.at[c], conv_sem.at[i]))
        copies[-1].start()
    for i in range(PIECES):
        loads[i].wait()
        stress[part(i), :] = (scaled[part(i), :] * factor_ref[0:1, :]).astype(bf16)
        copies.append(pltpu.make_async_copy(stress.at[part(i)], stress_out.at[part(i)], out_sem.at[i]))
        copies[-1].start()
    for copy in copies:
        copy.wait()


def shards(coefficients):
    tables = all_tables()
    hbm = pl.BlockSpec(memory_space=pl.ANY)
    vmem = pl.BlockSpec(memory_space=pltpu.VMEM)
    smem = pl.BlockSpec(memory_space=pltpu.SMEM)
    flat = [FLAT, HALF]
    shell = [NZ, FLAT]
    plane = [NT, 3 * HALF]
    semaphore = pltpu.SemaphoreType.DMA
    scratch = [
        (flat, f32), (flat, f32), (flat, bf16), (flat, bf16), (flat, bf16), (flat, bf16),
        (shell, f32), (shell, f32), (shell, f32), (shell, f32), (shell, f32), (shell, f32),
        (plane, f32), (plane, f32), (plane, f32), (plane, bf16), (plane, bf16),
        ([3 * NZ, NT], bf16), ([3 * NZ, NT], bf16), ([3 * NZ, NT], f32),
        ([FIELDS * NZ, NT], bf16), ([FIELDS * NZ, NT], bf16),
        ([FIELDS * KEPT, NT], bf16), ([FIELDS * KEPT, NT], bf16), ([FIELDS * KEPT, NT], bf16), ([FIELDS * KEPT, NT], bf16),
        ([FIELDS * NZ, NT], f32), ([6 * NT, HALF], f32), (flat, f32), (plane, f32),
        ([8, 128], f32), ([NZ, 128], f32),
        ([NT, NT], bf16), ([NT, NT], bf16), ([NT, NT], bf16), ([NT, NT], bf16),
    ]
    inverse = tables["inverse"]
    rows = np.zeros((8, HALF), np.float32)
    rows[:2] = inverse.reshape(2, HALF)
    operands = [coefficients.reshape(FLAT, HALF)]
    specs = [hbm]
    for name, spec in (("cheb", vmem), ("angle", hbm), ("smooth", hbm), ("axis", vmem), ("modes", vmem), ("modes_t", vmem)):
        operands += [jnp.asarray(part) for part in tables[name]]
        specs += [spec, spec]
    operands += [jnp.asarray(rows), jnp.asarray(inverse)]
    specs += [vmem, smem]
    conv, scaled, factor = pl.pallas_call(
        kernel,
        out_shape=(jax.ShapeDtypeStruct((FLAT, HALF), f32), jax.ShapeDtypeStruct((6 * NT, HALF), f32),
                   jax.ShapeDtypeStruct((8, HALF), f32)),
        in_specs=specs,
        out_specs=(hbm, hbm, vmem),
        scratch_shapes=[pltpu.VMEM(tuple(shape), kind) for shape, kind in scratch]
        + [semaphore((4,)), semaphore, semaphore((2,)), semaphore((3,)), semaphore((3,))]
        + [semaphore((3,)), semaphore((3,)), semaphore, semaphore]
        + [semaphore((3,)), semaphore((3,)), semaphore, semaphore]
        + [pltpu.SemaphoreType.REGULAR] * 2,
        compiler_params=pltpu.CompilerParams(collective_id=0, has_side_effects=True, vmem_limit_bytes=60 << 20),
    )(*operands)
    convection, stress = pl.pallas_call(
        finish,
        out_shape=(jax.ShapeDtypeStruct((FLAT, HALF), f32), jax.ShapeDtypeStruct((6 * NT, HALF), bf16)),
        in_specs=[hbm, hbm, vmem],
        out_specs=(hbm, hbm),
        scratch_shapes=[
            pltpu.VMEM((FLAT, HALF), f32),
            pltpu.VMEM((6 * NT, HALF), f32),
            pltpu.VMEM((6 * NT, HALF), bf16),
            semaphore((3,)),
            semaphore((3,)),
            semaphore((PIECES,)),
            semaphore((PIECES,)),
        ],
        compiler_params=pltpu.CompilerParams(vmem_limit_bytes=60 << 20),
    )(conv, scaled, factor)
    return (convection.reshape(3, 1, NT, HALF), stress.reshape(6, 1, NT, HALF))


def solution(mesh):
    return jax.shard_map(
        shards,
        mesh=mesh,
        in_specs=(P(None, "plane", None, "rad"),),
        out_specs=(P(None, "plane", None, "rad"), P(None, "plane", None, "rad")),
        check_vma=False,
    )
```

```python
import functools

import jax
import jax.numpy as jnp
import ml_dtypes
import numpy as np
from jax import lax
from jax.experimental import pallas as pl
from jax.experimental.pallas import tpu as pltpu
from jax.sharding import PartitionSpec as P

NZ = 128
NT = 768
NR = 256
HALF = 128
FLAT = 3 * NT
KEPT = 64
PIECES = 6
FIELDS = 21
EARLY = 12
early_strain = (1, 2, 5)
late_strain = (0, 3, 4)
strain_places = (12, 9, 10, 13, 14, 11)

inner_radius = 1.0
outer_radius = 1.4
axial_factor = 3.0
step_time = 0.002
component_pairs = ((0, 0), (1, 1), (2, 2), (0, 1), (0, 2), (1, 2))
pair_weights = (1.0, 1.0, 1.0, 2.0, 2.0, 2.0)

MESH = pl.DeviceIdType.MESH
f32 = jnp.float32
bf16 = jnp.bfloat16


def two_parts(table):
    table = table.astype(np.float32)
    high = table.astype(ml_dtypes.bfloat16)
    low = (table - high.astype(np.float32)).astype(ml_dtypes.bfloat16)
    return (high, low)


def chebyshev_tables(points):
    degree = np.arange(points, dtype=np.int64)
    angles = np.pi * np.mod(degree[:, None] * degree[None, :], 2 * (points - 1)) / (points - 1)
    node_angles = np.pi * degree / (points - 1)
    inside = (degree > 0) & (degree < points - 1)
    sines = np.where(inside, np.sin(node_angles), 1.0)
    real = degree.astype(np.float64)[:, None]
    parity = np.where(degree % 2 == 0, -1.0, 1.0)[:, None]
    edges = np.where(degree[None, :] == 0, real * real, parity * real * real)
    half_gap = 0.5 * (outer_radius - inner_radius)
    slopes = np.where(inside[None, :], real * np.sin(angles) / sines[None, :], edges) / half_gap
    radius = 0.5 * (inner_radius + outer_radius) + half_gap * np.cos(node_angles)
    return (np.cos(angles), slopes, radius)


def slope_table(points, factor):
    offset = np.arange(points)[:, None] - np.arange(points)[None, :]
    turned = np.pi * offset / points
    diagonal = offset == 0
    sines = np.where(diagonal, 1.0, np.sin(turned))
    parity = np.where(offset % 2 == 0, 0.5, -0.5)
    return np.where(diagonal, 0.0, factor * parity * np.cos(turned) / sines)


def smooth_table(points, keep):
    offset = np.arange(points)[:, None] - np.arange(points)[None, :]
    modes = np.arange(1, keep)
    row = (1.0 + 2.0 * np.cos(2 * np.pi * np.arange(points)[:, None] * modes / points).sum(1)) / points
    return row[np.mod(offset, points)]


def kept_modes(points, keep):
    place = 2 * np.pi * np.arange(points) / points
    table = np.zeros((points, 2 * keep))
    table[:, 0] = np.sqrt(1.0 / points)
    for mode in range(1, keep):
        table[:, 2 * mode - 1] = np.sqrt(2.0 / points) * np.cos(mode * place)
        table[:, 2 * mode] = np.sqrt(2.0 / points) * np.sin(mode * place)
    return table


def all_tables():
    values, slopes, radius = chebyshev_tables(NR)
    blocks = []
    for core in range(2):
        own = slice(core * HALF, (core + 1) * HALF)
        for part in range(2):
            degrees = slice(part * HALF, (part + 1) * HALF)
            blocks += [values[degrees, own].T, slopes[degrees, own].T]
    chebyshev = np.concatenate(blocks, 0)
    modes = kept_modes(NZ, NZ // 4)
    inverse = (1.0 / radius).astype(np.float32)
    return dict(
        cheb=two_parts(chebyshev),
        angle=two_parts(slope_table(NT, 1.0)),
        smooth=two_parts(smooth_table(NT, NT // 4)),
        axis=two_parts(slope_table(NZ, axial_factor)),
        modes=two_parts(modes),
        modes_t=two_parts(np.ascontiguousarray(modes.T)),
        inverse=inverse,
    )


def split(value):
    high = value.astype(bf16)
    return (high, (value - high.astype(f32)).astype(bf16))


def dot3(a, b, by_rows=False):
    dims = (((1,), (1 if by_rows else 0,)), ((), ()))
    one = functools.partial(lax.dot_general, dimension_numbers=dims, preferred_element_type=f32)
    return one(a[0], b[0]) + (one(a[0], b[1]) + one(a[1], b[0]))


def strain_of(velocity, radial, angular, axial, inverse):
    late = (None, None, None)
    if radial is not None:
        late = (
            radial[0],
            0.5 * (radial[1] + (angular[0] - velocity[1]) * inverse),
            0.5 * (axial[0] + radial[2]),
        )
    return (
        late[0],
        (angular[1] + velocity[0]) * inverse,
        axial[2],
        late[1],
        late[2],
        0.5 * (axial[1] + angular[2] * inverse),
    )


def magnitude_of(strain):
    straight = strain[0] * strain[0] + strain[1] * strain[1] + strain[2] * strain[2]
    mixed = strain[3] * strain[3] + strain[4] * strain[4] + strain[5] * strain[5]
    return jnp.sqrt(2.0 * (straight + 2.0 * mixed))


def flipped(value, mask, size):
    total, bit = 0, 1
    while bit < size:
        a, b = value // bit % 2, mask // bit % 2
        total = total + (a + b - 2 * a * b) * bit
        bit *= 2
    return total


def each_peer(me, core, body):
    own = me // 8
    for k in range(1, 8):
        body(own * 8 + flipped(me % 8, k + core * (8 - 2 * k), 8))
    low = [flipped(me % 8, k + core * (7 - 2 * k), 8) for k in range(8)]

    def group(i):
        first = flipped(own, i + 1 + core * (14 - 2 * i), 16) * 8
        for k in range(8):
            body(first + low[k])

    loop(NZ // 8 - 1, group)


def loop(count, body):
    def step(i, carry):
        body(i)
        return carry

    lax.fori_loop(0, count, step, 0)


def kernel(
    coef, cheb_h_hbm, cheb_l_hbm, angle_h_hbm, angle_l_hbm, smooth_h_hbm, smooth_l_hbm, axis_h_hbm, axis_l_hbm,
    modes_h_hbm, modes_l_hbm, modes_t_h_hbm, modes_t_l_hbm, inverse_rows_hbm, inverse_list_hbm,
    conv_out, scaled_out, factor_out,
    own, other, own_h, own_l, other_h, other_l, vel_t, rad_t, vel_z, rad_z, axial_z, axial_r, vel_p, rad_p, ang_p,
    vel_h, vel_l, vz_h, vz_l, ang_z, field_h, field_l, mode_h, mode_l, smoothed_h, smoothed_l, filtered, scaled, conv, axial_p,
    coefficient_own, coefficient_all, cheb_h, cheb_l, angle_h, angle_l, smooth_h, smooth_l, axis_h, axis_l, modes_h, modes_l,
    modes_t_h, modes_t_l, inverse_rows, inverse_list,
    table_sem, in_sem, out_sem, rad_send, rad_recv, vel_send, vel_recv, slope_send, slope_recv, back_send, back_recv,
    coefficient_send, coefficient_recv, in_y, in_x,
):
    me = lax.axis_index("plane")
    core = lax.axis_index("rad")
    partner = 1 - core

    x, y, z = me // 32, me // 8 % 4, me % 8
    along_z = [x * 32 + y * 8 + (z + k) % 8 for k in range(1, 8)]
    along_y = [x * 32 + (y + k) % 4 * 8 + z for k in range(1, 4)]
    along_x = [(x + k) % 4 * 32 + y * 8 + z for k in range(1, 4)]

    def greet(semaphore, places):
        for place in places:
            pl.semaphore_signal(semaphore, 1, device_id={"plane": place}, device_id_type=MESH)

    barrier = pltpu.get_barrier_semaphore()
    pl.semaphore_signal(barrier, 1, device_id={"rad": partner}, device_id_type=MESH)
    greet(barrier, along_z + along_y + along_x)
    load = pltpu.make_async_copy(coef, own, in_sem)
    load.start()
    sources = (
        cheb_h_hbm, cheb_l_hbm, angle_h_hbm, angle_l_hbm, smooth_h_hbm, smooth_l_hbm, axis_h_hbm, axis_l_hbm,
        modes_h_hbm, modes_l_hbm, modes_t_h_hbm, modes_t_l_hbm, inverse_rows_hbm, inverse_list_hbm,
    )
    places = (
        cheb_h, cheb_l, angle_h, angle_l, smooth_h, smooth_l, axis_h, axis_l, modes_h, modes_l, modes_t_h, modes_t_l,
        inverse_rows, inverse_list,
    )
    tables = [pltpu.make_async_copy(source, place, table_sem.at[i]) for i, (source, place) in enumerate(zip(sources, places))]
    for table in tables:
        table.start()
    pl.semaphore_wait(barrier, 14)
    exchanges = [
        pltpu.make_async_remote_copy(
            src_ref=coef.at[pl.ds(c * NT, NT)],
            dst_ref=other.at[pl.ds(c * NT, NT)],
            send_sem=rad_send.at[c],
            recv_sem=rad_recv.at[c],
            device_id={"rad": partner},
            device_id_type=MESH,
        )
        for c in range(3)
    ]
    for exchange in exchanges:
        exchange.start()
    greet(in_y, along_y)

    def cheb(part, first, rows):
        place = pl.ds(pl.multiple_of((core * 2 + part) * 256 + first, HALF), rows)
        return (cheb_h[place, :], cheb_l[place, :])

    def scatter(source, target, send, recv, lanes=slice(None)):
        local = pltpu.make_async_copy(source.at[pl.ds(me, 1), lanes], target.at[pl.ds(me, 1), lanes], recv)
        local.start()

        def one(d):
            pltpu.make_async_remote_copy(
                src_ref=source.at[pl.ds(d, 1), lanes],
                dst_ref=target.at[pl.ds(me, 1), lanes],
                send_sem=send,
                recv_sem=recv,
                device_id={"plane": d},
                device_id_type=MESH,
            ).start()

        each_peer(me, core, one)

    def wait_all(target, recv):
        pltpu.make_async_copy(target, target, recv).wait()

    def wait_sent(source, send):
        most = source.at[pl.ds(0, NZ - 8)]
        pltpu.make_async_copy(most, most, send).wait()
        last = source.at[pl.ds(0, 1)]
        for _ in range(7):
            pltpu.make_async_copy(last, last, send).wait()

    load.wait()
    tables[0].wait()
    tables[1].wait()

    def own_part(i):
        rows = pl.ds(pl.multiple_of(i * 256, 256), 256)
        part = split(own[rows, :])
        own_h[rows, :], own_l[rows, :] = part
        result = dot3(cheb(core, 0, 256), part, True)
        vel_t[:, rows] = result[:HALF]
        rad_t[:, rows] = result[HALF:]

    loop(3, own_part)
    pl.semaphore_wait(in_y, 3)
    greet(in_x, along_x)
    loop(6, lambda i: own_part(i + 3))

    def other_velocity(i):
        rows = pl.ds(pl.multiple_of(i * 256, 256), 256)
        part = split(other[rows, :])
        other_h[rows, :], other_l[rows, :] = part
        vel_t[:, rows] += dot3(cheb(partner, 0, HALF), part, True)

    for c in range(3):
        exchanges[c].wait_recv()
        loop(3, lambda i, c=c: other_velocity(i + 3 * c))
        if c == 0:
            pl.semaphore_wait(in_x, 3)
        scatter(vel_t, vel_z, vel_send.at[c], vel_recv.at[c], pl.ds(c * NT, NT))

    def other_slope(i):
        rows = pl.ds(pl.multiple_of(i * 256, 256), 256)
        rad_t[:, rows] += dot3(cheb(partner, HALF, HALF), (other_h[rows, :], other_l[rows, :]), True)

    loop(9, other_slope)
    scatter(rad_t, rad_z, slope_send, slope_recv)

    for c in range(3):
        lanes = slice(c * HALF, (c + 1) * HALF)

        def plane_part(i, c=c, lanes=lanes):
            rows = pl.ds(pl.multiple_of(c * NT + i * 256, 256), 256)
            place = pl.ds(pl.multiple_of(i * 256, 256), 256)
            result = dot3((own_h[rows, :], own_l[rows, :]), cheb(core, 0, 256), True)
            result += dot3((other_h[rows, :], other_l[rows, :]), cheb(partner, 0, 256), True)
            vel_p[place, lanes] = result[:, :HALF]
            rad_p[place, lanes] = result[:, HALF:]
            vel_h[place, lanes], vel_l[place, lanes] = split(result[:, :HALF])

        loop(3, plane_part)

    for table in tables[2:]:
        table.wait()

    def plane_angle(i):
        rows = pl.ds(pl.multiple_of(i * 256, 256), 256)
        ang_p[rows, :] = dot3((angle_h[rows, :], angle_l[rows, :]), (vel_h[...], vel_l[...]))

    loop(3, plane_angle)

    for c in range(3):
        wait_all(vel_z.at[:, pl.ds(c * NT, NT)], vel_recv.at[c])

        def axial_part(block, c=c):
            lanes = pl.ds(pl.multiple_of(c * NT + block * 256, 256), 256)
            part = split(vel_z[:, lanes])
            place = pl.ds(pl.multiple_of(block * 256, 256), 256)
            vz_h[c * NZ : (c + 1) * NZ, place], vz_l[c * NZ : (c + 1) * NZ, place] = part
            place = pl.ds(pl.multiple_of(block * NT + c * 256, 256), 256)
            axial_z[:, place] = dot3((axis_h[...], axis_l[...]), part)

        loop(3, axial_part)
    for block in range(3):
        scatter(axial_z, axial_r, back_send.at[block], back_recv.at[block], pl.ds(block * NT, NT))

    def shell_angle(i):
        lanes = pl.ds(pl.multiple_of(i * 256, 256), 256)
        ang_z[:, lanes] = -dot3((vz_h[...], vz_l[...]), (angle_h[:, lanes], angle_l[:, lanes]))

    loop(3, shell_angle)
    inverse = inverse_list[pl.ds(core * HALF + me, 1), :]

    def shell_block(i, block):
        rows = pl.ds(pl.multiple_of(i * 16, 16), 16)
        lanes = slice(block * 256, (block + 1) * 256)
        flat = [slice(c * NT + block * 256, c * NT + (block + 1) * 256) for c in range(3)]
        velocity = [vel_z[rows, flat[c]] for c in range(3)]
        axial = [axial_z[rows, block * NT + c * 256 : block * NT + (c + 1) * 256] for c in range(3)]
        angular = [ang_z[pl.ds(pl.multiple_of(c * NZ + i * 16, 16), 16), lanes] for c in range(3)]
        return rows, lanes, flat, velocity, axial, angular

    def keep(i, lanes, first, fields):
        for f, field in enumerate(fields):
            place = pl.ds(pl.multiple_of((first + f) * NZ + i * 16, 16), 16)
            field_h[place, lanes], field_l[place, lanes] = split(field)

    def early_products(i):
        for block in range(3):
            rows, lanes, flat, velocity, axial, angular = shell_block(i, block)
            strain = strain_of(velocity, None, angular, axial, inverse)
            pairs = [velocity[a] * velocity[b] for a, b in component_pairs]
            keep(i, lanes, 0, velocity + pairs + [strain[n] for n in early_strain])

    def late_products(i):
        for block in range(3):
            rows, lanes, flat, velocity, axial, angular = shell_block(i, block)
            radial = [rad_z[rows, flat[c]] for c in range(3)]
            strain = strain_of(velocity, radial, angular, axial, inverse)
            magnitude = magnitude_of(strain)
            keep(i, lanes, EARLY, [strain[n] for n in late_strain] + [magnitude * s for s in strain])

    def to_modes(f):
        rows = pl.ds(pl.multiple_of(f * NZ, NZ), NZ)
        place = pl.ds(pl.multiple_of(f * KEPT, KEPT), KEPT)
        for block in range(3):
            lanes = slice(block * 256, (block + 1) * 256)
            result = dot3((modes_t_h[...], modes_t_l[...]), (field_h[rows, lanes], field_l[rows, lanes]))
            mode_h[place, lanes], mode_l[place, lanes] = split(result)

    def smooth_rows(first, size):
        rows = pl.ds(pl.multiple_of(first, 64), size)
        for block in range(3):
            lanes = slice(block * 256, (block + 1) * 256)
            result = dot3((mode_h[rows, :], mode_l[rows, :]), (smooth_h[:, lanes], smooth_l[:, lanes]))
            smoothed_h[rows, lanes], smoothed_l[rows, lanes] = split(result)

    def from_modes(f):
        rows = pl.ds(pl.multiple_of(f * NZ, NZ), NZ)
        place = pl.ds(pl.multiple_of(f * KEPT, KEPT), KEPT)
        for block in range(3):
            lanes = slice(block * 256, (block + 1) * 256)
            filtered[rows, lanes] = dot3((modes_h[...], modes_l[...]), (smoothed_h[place, lanes], smoothed_l[place, lanes]))

    loop(NZ // 16, early_products)
    loop(EARLY, to_modes)
    loop(2, lambda g: smooth_rows(g * 384, 384))
    loop(EARLY, from_modes)
    wait_all(rad_z, slope_recv)
    loop(NZ // 16, late_products)
    loop(FIELDS - EARLY, lambda f: to_modes(EARLY + f))
    loop(3, lambda g: smooth_rows(EARLY * KEPT + g * 192, 192))
    loop(FIELDS - EARLY, lambda f: from_modes(EARLY + f))

    def shell_sums(i, sums):
        cross, model_sum = sums
        for block in range(3):
            lanes = slice(block * 256, (block + 1) * 256)
            mean = [filtered[pl.ds(pl.multiple_of(f * NZ + i * 8, 8), 8), lanes] for f in range(FIELDS)]
            strain = [mean[place] for place in strain_places]
            magnitude = magnitude_of(strain)
            for n, (a, b) in enumerate(component_pairs):
                leonard = mean[3 + n] - mean[a] * mean[b]
                model = 2.0 * (mean[15 + n] - 4.0 * (magnitude * strain[n]))
                weighted = model * pair_weights[n]
                cross = cross + leonard * weighted
                model_sum = model_sum + model * weighted
        return (cross, model_sum)

    zero = jnp.zeros((8, 256), f32)
    cross, model_sum = lax.fori_loop(0, NZ // 8, shell_sums, (zero, zero))

    def total(value):
        return jnp.sum(jnp.sum(value, axis=1, keepdims=True), axis=0, keepdims=True)

    points = NZ * NT
    coefficient = (total(cross) / points) / (total(model_sum) / points + 1e-06)
    coefficient_own[...] = jnp.broadcast_to(coefficient, (8, 128))

    def share(d):
        pltpu.make_async_remote_copy(
            src_ref=coefficient_own.at[pl.ds(0, 1)],
            dst_ref=coefficient_all.at[pl.ds(me, 1)],
            send_sem=coefficient_send,
            recv_sem=coefficient_recv,
            device_id={"plane": d},
            device_id_type=MESH,
        ).start()

    pltpu.make_async_copy(
        coefficient_own.at[pl.ds(0, 1)], coefficient_all.at[pl.ds(me, 1)], coefficient_recv
    ).start()
    each_peer(me, core, share)

    inverse_row = inverse_rows[pl.ds(core, 1), :]

    def plane_fields(i):
        rows = pl.ds(pl.multiple_of(i * 32, 32), 32)
        velocity, radial, angular, axial = (
            [ref[rows, c * HALF : (c + 1) * HALF] for c in range(3)] for ref in (vel_p, rad_p, ang_p, axial_p)
        )
        around = jnp.broadcast_to(inverse_row, (32, HALF))
        strain = strain_of(velocity, radial, angular, axial, around)
        magnitude = magnitude_of(strain)
        carried = velocity[1] * around
        parts = [velocity[0] * radial[c] + carried * angular[c] + velocity[2] * axial[c] for c in range(3)]
        parts[0] = parts[0] - velocity[1] * carried
        parts[1] = parts[1] + velocity[0] * carried
        for c in range(3):
            conv[pl.ds(pl.multiple_of(c * NT + i * 32, 32), 32), :] = -step_time * parts[c]
        for n in range(6):
            scaled[pl.ds(pl.multiple_of(n * NT + i * 32, 32), 32), :] = magnitude * strain[n]

    for block in range(3):
        arrived = axial_r.at[:, pl.ds(block * NT, NT)]
        wait_all(arrived, back_recv.at[block])
        for c in range(3):
            for half in range(2):
                first = block * NT + c * 256 + half * 128
                rows = slice(block * 256 + half * 128, block * 256 + (half + 1) * 128)
                axial_p[rows, c * HALF : (c + 1) * HALF] = axial_r[:, first : first + 128].T
        loop(8, lambda i, block=block: plane_fields(i + 8 * block))
        for n in range(3):
            rows = pl.ds(n * NT + block * 256, 256)
            pltpu.make_async_copy(conv.at[rows], conv_out.at[rows], out_sem.at[0]).start()
        for n in range(6):
            rows = pl.ds(n * NT + block * 256, 256)
            pltpu.make_async_copy(scaled.at[rows], scaled_out.at[rows], out_sem.at[1]).start()
    wait_all(coefficient_all, coefficient_recv)
    factor_out[...] = jnp.broadcast_to(-2.0 * coefficient_all[...].T[0:1, :], (8, HALF))

    for exchange in exchanges:
        exchange.wait_send()
    for c in range(3):
        wait_sent(vel_t.at[:, pl.ds(c * NT, NT)], vel_send.at[c])
    wait_sent(rad_t, slope_send)
    for block in range(3):
        wait_sent(axial_z.at[:, pl.ds(block * NT, NT)], back_send.at[block])
    wait_sent(coefficient_all, coefficient_send)
    pltpu.make_async_copy(conv, conv_out, out_sem.at[0]).wait()
    pltpu.make_async_copy(scaled, scaled_out, out_sem.at[1]).wait()


def finish(
    conv_ref, scaled_ref, factor_ref, conv_out, stress_out, conv, scaled, stress, conv_in_sem, conv_sem, in_sem, out_sem
):
    piece = 6 * NT // PIECES

    def part(i):
        return pl.ds(i * piece, piece)

    thirds = [pl.ds(c * NT, NT) for c in range(3)]
    loads = [pltpu.make_async_copy(scaled_ref.at[part(i)], scaled.at[part(i)], in_sem.at[i]) for i in range(PIECES)]
    moves = [pltpu.make_async_copy(conv_ref.at[c], conv.at[c], conv_in_sem.at[i]) for i, c in enumerate(thirds)]
    for copy in moves + loads:
        copy.start()
    copies = []
    for i, c in enumerate(thirds):
        moves[i].wait()
        copies.append(pltpu.make_async_copy(conv.at[c], conv_out.at[c], conv_sem.at[i]))
        copies[-1].start()
    for i in range(PIECES):
        loads[i].wait()
        stress[part(i), :] = (scaled[part(i), :] * factor_ref[0:1, :]).astype(bf16)
        copies.append(pltpu.make_async_copy(stress.at[part(i)], stress_out.at[part(i)], out_sem.at[i]))
        copies[-1].start()
    for copy in copies:
        copy.wait()


def shards(coefficients):
    tables = all_tables()
    hbm = pl.BlockSpec(memory_space=pl.ANY)
    vmem = pl.BlockSpec(memory_space=pltpu.VMEM)
    flat = [FLAT, HALF]
    shell = [NZ, FLAT]
    plane = [NT, 3 * HALF]
    semaphore = pltpu.SemaphoreType.DMA
    scratch = [
        (flat, f32), (flat, f32), (flat, bf16), (flat, bf16), (flat, bf16), (flat, bf16),
        (shell, f32), (shell, f32), (shell, f32), (shell, f32), (shell, f32), (shell, f32),
        (plane, f32), (plane, f32), (plane, f32), (plane, bf16), (plane, bf16),
        ([3 * NZ, NT], bf16), ([3 * NZ, NT], bf16), ([3 * NZ, NT], f32),
        ([FIELDS * NZ, NT], bf16), ([FIELDS * NZ, NT], bf16),
        ([FIELDS * KEPT, NT], bf16), ([FIELDS * KEPT, NT], bf16), ([FIELDS * KEPT, NT], bf16), ([FIELDS * KEPT, NT], bf16),
        ([FIELDS * NZ, NT], f32), ([6 * NT, HALF], f32), (flat, f32), (plane, f32),
        ([8, 128], f32), ([NZ, 128], f32),
        ([1024, HALF], bf16), ([1024, HALF], bf16),
        ([NT, NT], bf16), ([NT, NT], bf16), ([NT, NT], bf16), ([NT, NT], bf16),
        ([NZ, NZ], bf16), ([NZ, NZ], bf16), ([NZ, KEPT], bf16), ([NZ, KEPT], bf16), ([KEPT, NZ], bf16), ([KEPT, NZ], bf16),
        ([8, HALF], f32), ([NR, 256], f32),
    ]
    inverse = tables["inverse"]
    rows = np.zeros((8, HALF), np.float32)
    rows[:2] = inverse.reshape(2, HALF)
    operands = [coefficients.reshape(FLAT, HALF)]
    for name in ("cheb", "angle", "smooth", "axis", "modes", "modes_t"):
        operands += [jnp.asarray(part) for part in tables[name]]
    operands += [jnp.asarray(rows), jnp.asarray(np.broadcast_to(inverse[:, None], (NR, 256)).copy())]
    specs = [hbm] * len(operands)
    conv, scaled, factor = pl.pallas_call(
        kernel,
        out_shape=(jax.ShapeDtypeStruct((FLAT, HALF), f32), jax.ShapeDtypeStruct((6 * NT, HALF), f32),
                   jax.ShapeDtypeStruct((8, HALF), f32)),
        in_specs=specs,
        out_specs=(hbm, hbm, vmem),
        scratch_shapes=[pltpu.VMEM(tuple(shape), kind) for shape, kind in scratch]
        + [semaphore((14,)), semaphore, semaphore((2,)), semaphore((3,)), semaphore((3,))]
        + [semaphore((3,)), semaphore((3,)), semaphore, semaphore]
        + [semaphore((3,)), semaphore((3,)), semaphore, semaphore]
        + [pltpu.SemaphoreType.REGULAR] * 2,
        compiler_params=pltpu.CompilerParams(collective_id=0, has_side_effects=True, vmem_limit_bytes=60 << 20),
    )(*operands)
    convection, stress = pl.pallas_call(
        finish,
        out_shape=(jax.ShapeDtypeStruct((FLAT, HALF), f32), jax.ShapeDtypeStruct((6 * NT, HALF), bf16)),
        in_specs=[hbm, hbm, vmem],
        out_specs=(hbm, hbm),
        scratch_shapes=[
            pltpu.VMEM((FLAT, HALF), f32),
            pltpu.VMEM((6 * NT, HALF), f32),
            pltpu.VMEM((6 * NT, HALF), bf16),
            semaphore((3,)),
            semaphore((3,)),
            semaphore((PIECES,)),
            semaphore((PIECES,)),
        ],
        compiler_params=pltpu.CompilerParams(vmem_limit_bytes=60 << 20),
    )(conv, scaled, factor)
    return (convection.reshape(3, 1, NT, HALF), stress.reshape(6, 1, NT, HALF))


def solution(mesh):
    return jax.shard_map(
        shards,
        mesh=mesh,
        in_specs=(P(None, "plane", None, "rad"),),
        out_specs=(P(None, "plane", None, "rad"), P(None, "plane", None, "rad")),
        check_vma=False,
    )
```

```python
import functools

import jax
import jax.numpy as jnp
import ml_dtypes
import numpy as np
from jax import lax
from jax.experimental import pallas as pl
from jax.experimental.pallas import tpu as pltpu
from jax.sharding import PartitionSpec as P

NZ = 128
NT = 768
NR = 256
HALF = 128
FLAT = 3 * NT
KEPT = 64
PIECES = 6
FIELDS = 21
EARLY = 12
early_strain = (1, 2, 5)
late_strain = (0, 3, 4)
strain_places = (12, 9, 10, 13, 14, 11)

inner_radius = 1.0
outer_radius = 1.4
axial_factor = 3.0
step_time = 0.002
component_pairs = ((0, 0), (1, 1), (2, 2), (0, 1), (0, 2), (1, 2))
pair_weights = (1.0, 1.0, 1.0, 2.0, 2.0, 2.0)

MESH = pl.DeviceIdType.MESH
f32 = jnp.float32
bf16 = jnp.bfloat16


def two_parts(table):
    table = table.astype(np.float32)
    high = table.astype(ml_dtypes.bfloat16)
    low = (table - high.astype(np.float32)).astype(ml_dtypes.bfloat16)
    return (high, low)


def chebyshev_tables(points):
    degree = np.arange(points, dtype=np.int64)
    angles = np.pi * np.mod(degree[:, None] * degree[None, :], 2 * (points - 1)) / (points - 1)
    node_angles = np.pi * degree / (points - 1)
    inside = (degree > 0) & (degree < points - 1)
    sines = np.where(inside, np.sin(node_angles), 1.0)
    real = degree.astype(np.float64)[:, None]
    parity = np.where(degree % 2 == 0, -1.0, 1.0)[:, None]
    edges = np.where(degree[None, :] == 0, real * real, parity * real * real)
    half_gap = 0.5 * (outer_radius - inner_radius)
    slopes = np.where(inside[None, :], real * np.sin(angles) / sines[None, :], edges) / half_gap
    radius = 0.5 * (inner_radius + outer_radius) + half_gap * np.cos(node_angles)
    return (np.cos(angles), slopes, radius)


def slope_table(points, factor):
    offset = np.arange(points)[:, None] - np.arange(points)[None, :]
    turned = np.pi * offset / points
    diagonal = offset == 0
    sines = np.where(diagonal, 1.0, np.sin(turned))
    parity = np.where(offset % 2 == 0, 0.5, -0.5)
    return np.where(diagonal, 0.0, factor * parity * np.cos(turned) / sines)


def smooth_table(points, keep):
    offset = np.arange(points)[:, None] - np.arange(points)[None, :]
    modes = np.arange(1, keep)
    row = (1.0 + 2.0 * np.cos(2 * np.pi * np.arange(points)[:, None] * modes / points).sum(1)) / points
    return row[np.mod(offset, points)]


def kept_modes(points, keep):
    place = 2 * np.pi * np.arange(points) / points
    table = np.zeros((points, 2 * keep))
    table[:, 0] = np.sqrt(1.0 / points)
    for mode in range(1, keep):
        table[:, 2 * mode - 1] = np.sqrt(2.0 / points) * np.cos(mode * place)
        table[:, 2 * mode] = np.sqrt(2.0 / points) * np.sin(mode * place)
    return table


def all_tables():
    values, slopes, radius = chebyshev_tables(NR)
    blocks = []
    for core in range(2):
        own = slice(core * HALF, (core + 1) * HALF)
        for part in range(2):
            degrees = slice(part * HALF, (part + 1) * HALF)
            blocks += [values[degrees, own].T, slopes[degrees, own].T]
    chebyshev = np.concatenate(blocks, 0)
    modes = kept_modes(NZ, NZ // 4)
    inverse = (1.0 / radius).astype(np.float32)
    return dict(
        cheb=two_parts(chebyshev),
        angle=two_parts(slope_table(NT, 1.0)),
        smooth=two_parts(smooth_table(NT, NT // 4)),
        axis=two_parts(slope_table(NZ, axial_factor)),
        modes=two_parts(modes),
        modes_t=two_parts(np.ascontiguousarray(modes.T)),
        inverse=inverse,
    )


def split(value):
    high = value.astype(bf16)
    return (high, (value - high.astype(f32)).astype(bf16))


def dot3(a, b, by_rows=False):
    dims = (((1,), (1 if by_rows else 0,)), ((), ()))
    one = functools.partial(lax.dot_general, dimension_numbers=dims, preferred_element_type=f32)
    return one(a[0], b[0]) + (one(a[0], b[1]) + one(a[1], b[0]))


def strain_of(velocity, radial, angular, axial, inverse):
    late = (None, None, None)
    if radial is not None:
        late = (
            radial[0],
            0.5 * (radial[1] + (angular[0] - velocity[1]) * inverse),
            0.5 * (axial[0] + radial[2]),
        )
    return (
        late[0],
        (angular[1] + velocity[0]) * inverse,
        axial[2],
        late[1],
        late[2],
        0.5 * (axial[1] + angular[2] * inverse),
    )


def magnitude_of(strain):
    straight = strain[0] * strain[0] + strain[1] * strain[1] + strain[2] * strain[2]
    mixed = strain[3] * strain[3] + strain[4] * strain[4] + strain[5] * strain[5]
    return jnp.sqrt(2.0 * (straight + 2.0 * mixed))


def flipped(value, mask, size):
    total, bit = 0, 1
    while bit < size:
        a, b = value // bit % 2, mask // bit % 2
        total = total + (a + b - 2 * a * b) * bit
        bit *= 2
    return total


def each_peer(me, core, body):
    own = me // 8
    for k in range(1, 8):
        body(own * 8 + flipped(me % 8, k + core * (8 - 2 * k), 8))
    low = [flipped(me % 8, k + core * (7 - 2 * k), 8) for k in range(8)]

    def group(i):
        first = flipped(own, i + 1 + core * (14 - 2 * i), 16) * 8
        for k in range(8):
            body(first + low[k])

    loop(NZ // 8 - 1, group)


def loop(count, body):
    def step(i, carry):
        body(i)
        return carry

    lax.fori_loop(0, count, step, 0)


def kernel(
    coef, cheb_h_hbm, cheb_l_hbm, angle_h_hbm, angle_l_hbm, smooth_h_hbm, smooth_l_hbm, axis_h_hbm, axis_l_hbm,
    modes_h_hbm, modes_l_hbm, modes_t_h_hbm, modes_t_l_hbm, inverse_rows_hbm, inverse_list_hbm,
    conv_out, scaled_out, factor_out,
    own, other, own_h, own_l, other_h, other_l, vel_t, rad_t, vel_z, rad_z, axial_z, axial_r, vel_p, rad_p, ang_p,
    vel_h, vel_l, vz_h, vz_l, ang_z, field_h, field_l, mode_h, mode_l, smoothed_h, smoothed_l, filtered, scaled, conv, axial_p,
    coefficient_own, coefficient_all, cheb_h, cheb_l, angle_h, angle_l, smooth_h, smooth_l, axis_h, axis_l, modes_h, modes_l,
    modes_t_h, modes_t_l, inverse_rows, inverse_list,
    table_sem, in_sem, out_sem, rad_send, rad_recv, vel_send, vel_recv, slope_send, slope_recv, back_send, back_recv,
    coefficient_send, coefficient_recv, in_y, in_x,
):
    me = lax.axis_index("plane")
    core = lax.axis_index("rad")
    partner = 1 - core

    x, y, z = me // 32, me // 8 % 4, me % 8
    along_z = [x * 32 + y * 8 + (z + k) % 8 for k in range(1, 8)]
    along_y = [x * 32 + (y + k) % 4 * 8 + z for k in range(1, 4)]
    along_x = [(x + k) % 4 * 32 + y * 8 + z for k in range(1, 4)]

    def greet(semaphore, places):
        for place in places:
            pl.semaphore_signal(semaphore, 1, device_id={"plane": place}, device_id_type=MESH)

    barrier = pltpu.get_barrier_semaphore()
    pl.semaphore_signal(barrier, 1, device_id={"rad": partner}, device_id_type=MESH)
    greet(barrier, along_z + along_y + along_x)
    load = pltpu.make_async_copy(coef, own, in_sem)
    load.start()
    sources = (
        cheb_h_hbm, cheb_l_hbm, angle_h_hbm, angle_l_hbm, smooth_h_hbm, smooth_l_hbm, axis_h_hbm, axis_l_hbm,
        modes_h_hbm, modes_l_hbm, modes_t_h_hbm, modes_t_l_hbm, inverse_rows_hbm, inverse_list_hbm,
    )
    places = (
        cheb_h, cheb_l, angle_h, angle_l, smooth_h, smooth_l, axis_h, axis_l, modes_h, modes_l, modes_t_h, modes_t_l,
        inverse_rows, inverse_list,
    )
    tables = [pltpu.make_async_copy(source, place, table_sem.at[i]) for i, (source, place) in enumerate(zip(sources, places))]
    for table in tables:
        table.start()
    pl.semaphore_wait(barrier, 14)
    exchanges = [
        pltpu.make_async_remote_copy(
            src_ref=coef.at[pl.ds(c * NT, NT)],
            dst_ref=other.at[pl.ds(c * NT, NT)],
            send_sem=rad_send.at[c],
            recv_sem=rad_recv.at[c],
            device_id={"rad": partner},
            device_id_type=MESH,
        )
        for c in range(3)
    ]
    for exchange in exchanges:
        exchange.start()
    greet(in_y, along_y)

    def cheb(part, first, rows):
        place = pl.ds(pl.multiple_of((core * 2 + part) * 256 + first, HALF), rows)
        return (cheb_h[place, :], cheb_l[place, :])

    def scatter(source, target, send, recv, lanes=slice(None)):
        local = pltpu.make_async_copy(source.at[pl.ds(me, 1), lanes], target.at[pl.ds(me, 1), lanes], recv)
        local.start()

        def one(d):
            pltpu.make_async_remote_copy(
                src_ref=source.at[pl.ds(d, 1), lanes],
                dst_ref=target.at[pl.ds(me, 1), lanes],
                send_sem=send,
                recv_sem=recv,
                device_id={"plane": d},
                device_id_type=MESH,
            ).start()

        each_peer(me, core, one)

    def wait_all(target, recv):
        pltpu.make_async_copy(target, target, recv).wait()

    def wait_sent(source, send):
        most = source.at[pl.ds(0, NZ - 8)]
        pltpu.make_async_copy(most, most, send).wait()
        last = source.at[pl.ds(0, 1)]
        for _ in range(7):
            pltpu.make_async_copy(last, last, send).wait()

    load.wait()
    tables[0].wait()
    tables[1].wait()

    def own_velocity(i):
        rows = pl.ds(pl.multiple_of(i * 256, 256), 256)
        part = split(own[rows, :])
        own_h[rows, :], own_l[rows, :] = part
        vel_t[:, rows] = dot3(cheb(core, 0, HALF), part, True)

    def other_velocity(i):
        rows = pl.ds(pl.multiple_of(i * 256, 256), 256)
        part = split(other[rows, :])
        other_h[rows, :], other_l[rows, :] = part
        vel_t[:, rows] += dot3(cheb(partner, 0, HALF), part, True)

    for c in range(3):
        loop(3, lambda i, c=c: own_velocity(i + 3 * c))
        if c == 0:
            pl.semaphore_wait(in_y, 3)
            greet(in_x, along_x)
        exchanges[c].wait_recv()
        loop(3, lambda i, c=c: other_velocity(i + 3 * c))
        if c == 0:
            pl.semaphore_wait(in_x, 3)
        scatter(vel_t, vel_z, vel_send.at[c], vel_recv.at[c], pl.ds(c * NT, NT))

    def both_slopes(i):
        rows = pl.ds(pl.multiple_of(i * 256, 256), 256)
        result = dot3(cheb(core, HALF, HALF), (own_h[rows, :], own_l[rows, :]), True)
        rad_t[:, rows] = result + dot3(cheb(partner, HALF, HALF), (other_h[rows, :], other_l[rows, :]), True)

    loop(9, both_slopes)
    scatter(rad_t, rad_z, slope_send, slope_recv)

    for c in range(3):
        lanes = slice(c * HALF, (c + 1) * HALF)

        def plane_part(i, c=c, lanes=lanes):
            rows = pl.ds(pl.multiple_of(c * NT + i * 256, 256), 256)
            place = pl.ds(pl.multiple_of(i * 256, 256), 256)
            result = dot3((own_h[rows, :], own_l[rows, :]), cheb(core, 0, 256), True)
            result += dot3((other_h[rows, :], other_l[rows, :]), cheb(partner, 0, 256), True)
            vel_p[place, lanes] = result[:, :HALF]
            rad_p[place, lanes] = result[:, HALF:]
            vel_h[place, lanes], vel_l[place, lanes] = split(result[:, :HALF])

        loop(3, plane_part)

    for table in tables[2:]:
        table.wait()

    def plane_angle(i):
        rows = pl.ds(pl.multiple_of(i * 256, 256), 256)
        ang_p[rows, :] = dot3((angle_h[rows, :], angle_l[rows, :]), (vel_h[...], vel_l[...]))

    loop(3, plane_angle)

    for c in range(3):
        wait_all(vel_z.at[:, pl.ds(c * NT, NT)], vel_recv.at[c])

        def axial_part(block, c=c):
            lanes = pl.ds(pl.multiple_of(c * NT + block * 256, 256), 256)
            part = split(vel_z[:, lanes])
            place = pl.ds(pl.multiple_of(block * 256, 256), 256)
            vz_h[c * NZ : (c + 1) * NZ, place], vz_l[c * NZ : (c + 1) * NZ, place] = part
            place = pl.ds(pl.multiple_of(block * NT + c * 256, 256), 256)
            axial_z[:, place] = dot3((axis_h[...], axis_l[...]), part)

        loop(3, axial_part)
    for block in range(3):
        scatter(axial_z, axial_r, back_send.at[block], back_recv.at[block], pl.ds(block * NT, NT))

    def shell_angle(i):
        lanes = pl.ds(pl.multiple_of(i * 256, 256), 256)
        ang_z[:, lanes] = -dot3((vz_h[...], vz_l[...]), (angle_h[:, lanes], angle_l[:, lanes]))

    loop(3, shell_angle)
    inverse = inverse_list[pl.ds(core * HALF + me, 1), :]

    def shell_block(i, block):
        rows = pl.ds(pl.multiple_of(i * 16, 16), 16)
        lanes = slice(block * 256, (block + 1) * 256)
        flat = [slice(c * NT + block * 256, c * NT + (block + 1) * 256) for c in range(3)]
        velocity = [vel_z[rows, flat[c]] for c in range(3)]
        axial = [axial_z[rows, block * NT + c * 256 : block * NT + (c + 1) * 256] for c in range(3)]
        angular = [ang_z[pl.ds(pl.multiple_of(c * NZ + i * 16, 16), 16), lanes] for c in range(3)]
        return rows, lanes, flat, velocity, axial, angular

    def keep(i, lanes, first, fields):
        for f, field in enumerate(fields):
            place = pl.ds(pl.multiple_of((first + f) * NZ + i * 16, 16), 16)
            field_h[place, lanes], field_l[place, lanes] = split(field)

    def early_products(i):
        for block in range(3):
            rows, lanes, flat, velocity, axial, angular = shell_block(i, block)
            strain = strain_of(velocity, None, angular, axial, inverse)
            pairs = [velocity[a] * velocity[b] for a, b in component_pairs]
            keep(i, lanes, 0, velocity + pairs + [strain[n] for n in early_strain])

    def late_products(i):
        for block in range(3):
            rows, lanes, flat, velocity, axial, angular = shell_block(i, block)
            radial = [rad_z[rows, flat[c]] for c in range(3)]
            strain = strain_of(velocity, radial, angular, axial, inverse)
            magnitude = magnitude_of(strain)
            keep(i, lanes, EARLY, [strain[n] for n in late_strain] + [magnitude * s for s in strain])

    def to_modes(f):
        rows = pl.ds(pl.multiple_of(f * NZ, NZ), NZ)
        place = pl.ds(pl.multiple_of(f * KEPT, KEPT), KEPT)
        for block in range(3):
            lanes = slice(block * 256, (block + 1) * 256)
            result = dot3((modes_t_h[...], modes_t_l[...]), (field_h[rows, lanes], field_l[rows, lanes]))
            mode_h[place, lanes], mode_l[place, lanes] = split(result)

    def smooth_rows(first, size):
        rows = pl.ds(pl.multiple_of(first, 64), size)
        for block in range(3):
            lanes = slice(block * 256, (block + 1) * 256)
            result = dot3((mode_h[rows, :], mode_l[rows, :]), (smooth_h[:, lanes], smooth_l[:, lanes]))
            smoothed_h[rows, lanes], smoothed_l[rows, lanes] = split(result)

    def from_modes(f):
        rows = pl.ds(pl.multiple_of(f * NZ, NZ), NZ)
        place = pl.ds(pl.multiple_of(f * KEPT, KEPT), KEPT)
        for block in range(3):
            lanes = slice(block * 256, (block + 1) * 256)
            filtered[rows, lanes] = dot3((modes_h[...], modes_l[...]), (smoothed_h[place, lanes], smoothed_l[place, lanes]))

    loop(NZ // 16, early_products)
    loop(EARLY, to_modes)
    loop(2, lambda g: smooth_rows(g * 384, 384))
    loop(EARLY, from_modes)
    wait_all(rad_z, slope_recv)
    loop(NZ // 16, late_products)
    loop(FIELDS - EARLY, lambda f: to_modes(EARLY + f))
    loop(3, lambda g: smooth_rows(EARLY * KEPT + g * 192, 192))
    loop(FIELDS - EARLY, lambda f: from_modes(EARLY + f))

    def shell_sums(i, sums):
        cross, model_sum = sums
        for block in range(3):
            lanes = slice(block * 256, (block + 1) * 256)
            mean = [filtered[pl.ds(pl.multiple_of(f * NZ + i * 8, 8), 8), lanes] for f in range(FIELDS)]
            strain = [mean[place] for place in strain_places]
            magnitude = magnitude_of(strain)
            for n, (a, b) in enumerate(component_pairs):
                leonard = mean[3 + n] - mean[a] * mean[b]
                model = 2.0 * (mean[15 + n] - 4.0 * (magnitude * strain[n]))
                weighted = model * pair_weights[n]
                cross = cross + leonard * weighted
                model_sum = model_sum + model * weighted
        return (cross, model_sum)

    zero = jnp.zeros((8, 256), f32)
    cross, model_sum = lax.fori_loop(0, NZ // 8, shell_sums, (zero, zero))

    def total(value):
        return jnp.sum(jnp.sum(value, axis=1, keepdims=True), axis=0, keepdims=True)

    points = NZ * NT
    coefficient = (total(cross) / points) / (total(model_sum) / points + 1e-06)
    coefficient_own[...] = jnp.broadcast_to(coefficient, (8, 128))

    def share(d):
        pltpu.make_async_remote_copy(
            src_ref=coefficient_own.at[pl.ds(0, 1)],
            dst_ref=coefficient_all.at[pl.ds(me, 1)],
            send_sem=coefficient_send,
            recv_sem=coefficient_recv,
            device_id={"plane": d},
            device_id_type=MESH,
        ).start()

    pltpu.make_async_copy(
        coefficient_own.at[pl.ds(0, 1)], coefficient_all.at[pl.ds(me, 1)], coefficient_recv
    ).start()
    each_peer(me, core, share)

    inverse_row = inverse_rows[pl.ds(core, 1), :]

    def plane_fields(i):
        rows = pl.ds(pl.multiple_of(i * 32, 32), 32)
        velocity, radial, angular, axial = (
            [ref[rows, c * HALF : (c + 1) * HALF] for c in range(3)] for ref in (vel_p, rad_p, ang_p, axial_p)
        )
        around = jnp.broadcast_to(inverse_row, (32, HALF))
        strain = strain_of(velocity, radial, angular, axial, around)
        magnitude = magnitude_of(strain)
        carried = velocity[1] * around
        parts = [velocity[0] * radial[c] + carried * angular[c] + velocity[2] * axial[c] for c in range(3)]
        parts[0] = parts[0] - velocity[1] * carried
        parts[1] = parts[1] + velocity[0] * carried
        for c in range(3):
            conv[pl.ds(pl.multiple_of(c * NT + i * 32, 32), 32), :] = -step_time * parts[c]
        for n in range(6):
            scaled[pl.ds(pl.multiple_of(n * NT + i * 32, 32), 32), :] = magnitude * strain[n]

    for block in range(3):
        arrived = axial_r.at[:, pl.ds(block * NT, NT)]
        wait_all(arrived, back_recv.at[block])
        for c in range(3):
            for half in range(2):
                first = block * NT + c * 256 + half * 128
                rows = slice(block * 256 + half * 128, block * 256 + (half + 1) * 128)
                axial_p[rows, c * HALF : (c + 1) * HALF] = axial_r[:, first : first + 128].T
        loop(8, lambda i, block=block: plane_fields(i + 8 * block))
        for n in range(3):
            rows = pl.ds(n * NT + block * 256, 256)
            pltpu.make_async_copy(conv.at[rows], conv_out.at[rows], out_sem.at[0]).start()
        for n in range(6):
            rows = pl.ds(n * NT + block * 256, 256)
            pltpu.make_async_copy(scaled.at[rows], scaled_out.at[rows], out_sem.at[1]).start()
    wait_all(coefficient_all, coefficient_recv)
    factor_out[...] = jnp.broadcast_to(-2.0 * coefficient_all[...].T[0:1, :], (8, HALF))

    for exchange in exchanges:
        exchange.wait_send()
    for c in range(3):
        wait_sent(vel_t.at[:, pl.ds(c * NT, NT)], vel_send.at[c])
    wait_sent(rad_t, slope_send)
    for block in range(3):
        wait_sent(axial_z.at[:, pl.ds(block * NT, NT)], back_send.at[block])
    wait_sent(coefficient_all, coefficient_send)
    pltpu.make_async_copy(conv, conv_out, out_sem.at[0]).wait()
    pltpu.make_async_copy(scaled, scaled_out, out_sem.at[1]).wait()


def finish(
    conv_ref, scaled_ref, factor_ref, conv_out, stress_out, conv, scaled, stress, conv_in_sem, conv_sem, in_sem, out_sem
):
    piece = 6 * NT // PIECES

    def part(i):
        return pl.ds(i * piece, piece)

    thirds = [pl.ds(c * NT, NT) for c in range(3)]
    loads = [pltpu.make_async_copy(scaled_ref.at[part(i)], scaled.at[part(i)], in_sem.at[i]) for i in range(PIECES)]
    moves = [pltpu.make_async_copy(conv_ref.at[c], conv.at[c], conv_in_sem.at[i]) for i, c in enumerate(thirds)]
    for copy in moves + loads:
        copy.start()
    copies = []
    for i, c in enumerate(thirds):
        moves[i].wait()
        copies.append(pltpu.make_async_copy(conv.at[c], conv_out.at[c], conv_sem.at[i]))
        copies[-1].start()
    for i in range(PIECES):
        loads[i].wait()
        stress[part(i), :] = (scaled[part(i), :] * factor_ref[0:1, :]).astype(bf16)
        copies.append(pltpu.make_async_copy(stress.at[part(i)], stress_out.at[part(i)], out_sem.at[i]))
        copies[-1].start()
    for copy in copies:
        copy.wait()


def shards(coefficients):
    tables = all_tables()
    hbm = pl.BlockSpec(memory_space=pl.ANY)
    vmem = pl.BlockSpec(memory_space=pltpu.VMEM)
    flat = [FLAT, HALF]
    shell = [NZ, FLAT]
    plane = [NT, 3 * HALF]
    semaphore = pltpu.SemaphoreType.DMA
    scratch = [
        (flat, f32), (flat, f32), (flat, bf16), (flat, bf16), (flat, bf16), (flat, bf16),
        (shell, f32), (shell, f32), (shell, f32), (shell, f32), (shell, f32), (shell, f32),
        (plane, f32), (plane, f32), (plane, f32), (plane, bf16), (plane, bf16),
        ([3 * NZ, NT], bf16), ([3 * NZ, NT], bf16), ([3 * NZ, NT], f32),
        ([FIELDS * NZ, NT], bf16), ([FIELDS * NZ, NT], bf16),
        ([FIELDS * KEPT, NT], bf16), ([FIELDS * KEPT, NT], bf16), ([FIELDS * KEPT, NT], bf16), ([FIELDS * KEPT, NT], bf16),
        ([FIELDS * NZ, NT], f32), ([6 * NT, HALF], f32), (flat, f32), (plane, f32),
        ([8, 128], f32), ([NZ, 128], f32),
        ([1024, HALF], bf16), ([1024, HALF], bf16),
        ([NT, NT], bf16), ([NT, NT], bf16), ([NT, NT], bf16), ([NT, NT], bf16),
        ([NZ, NZ], bf16), ([NZ, NZ], bf16), ([NZ, KEPT], bf16), ([NZ, KEPT], bf16), ([KEPT, NZ], bf16), ([KEPT, NZ], bf16),
        ([8, HALF], f32), ([NR, 256], f32),
    ]
    inverse = tables["inverse"]
    rows = np.zeros((8, HALF), np.float32)
    rows[:2] = inverse.reshape(2, HALF)
    operands = [coefficients.reshape(FLAT, HALF)]
    for name in ("cheb", "angle", "smooth", "axis", "modes", "modes_t"):
        operands += [jnp.asarray(part) for part in tables[name]]
    operands += [jnp.asarray(rows), jnp.asarray(np.broadcast_to(inverse[:, None], (NR, 256)).copy())]
    specs = [hbm] * len(operands)
    conv, scaled, factor = pl.pallas_call(
        kernel,
        out_shape=(jax.ShapeDtypeStruct((FLAT, HALF), f32), jax.ShapeDtypeStruct((6 * NT, HALF), f32),
                   jax.ShapeDtypeStruct((8, HALF), f32)),
        in_specs=specs,
        out_specs=(hbm, hbm, vmem),
        scratch_shapes=[pltpu.VMEM(tuple(shape), kind) for shape, kind in scratch]
        + [semaphore((14,)), semaphore, semaphore((2,)), semaphore((3,)), semaphore((3,))]
        + [semaphore((3,)), semaphore((3,)), semaphore, semaphore]
        + [semaphore((3,)), semaphore((3,)), semaphore, semaphore]
        + [pltpu.SemaphoreType.REGULAR] * 2,
        compiler_params=pltpu.CompilerParams(collective_id=0, has_side_effects=True, vmem_limit_bytes=60 << 20),
    )(*operands)
    convection, stress = pl.pallas_call(
        finish,
        out_shape=(jax.ShapeDtypeStruct((FLAT, HALF), f32), jax.ShapeDtypeStruct((6 * NT, HALF), bf16)),
        in_specs=[hbm, hbm, vmem],
        out_specs=(hbm, hbm),
        scratch_shapes=[
            pltpu.VMEM((FLAT, HALF), f32),
            pltpu.VMEM((6 * NT, HALF), f32),
            pltpu.VMEM((6 * NT, HALF), bf16),
            semaphore((3,)),
            semaphore((3,)),
            semaphore((PIECES,)),
            semaphore((PIECES,)),
        ],
        compiler_params=pltpu.CompilerParams(vmem_limit_bytes=60 << 20),
    )(conv, scaled, factor)
    return (convection.reshape(3, 1, NT, HALF), stress.reshape(6, 1, NT, HALF))


def solution(mesh):
    return jax.shard_map(
        shards,
        mesh=mesh,
        in_specs=(P(None, "plane", None, "rad"),),
        out_specs=(P(None, "plane", None, "rad"), P(None, "plane", None, "rad")),
        check_vma=False,
    )
```
